256 devices in a mesh: heads: 32 (over z, x_lo, core), frames: 8 (over y, x_hi).
Axes of the slice: x: 4 (x_hi: 2, x_lo: 2; x = x_hi * 2 + x_lo), y: 4, z: 8, core: 2. Of those that a mesh axis runs over, the one named last changes fastest.
Arguments:
- query: bfloat16 [32768, 4096], P(('frames', 'heads'))
- keys: bfloat16 [32768, 4096], P(('frames', 'heads'))
- values: bfloat16 [32768, 4096], P(('frames', 'heads')), may hold values from -6 to 6
- query_tan: bfloat16 [32768, 4096], P(('frames', 'heads')), may hold values from -6 to 6
- keys_tan: bfloat16 [32768, 4096], P(('frames', 'heads')), may hold values from -6 to 6
- values_tan: bfloat16 [32768, 4096], P(('frames', 'heads')), may hold values from -6 to 6
- neighbors: int32 [128, 4], P('frames'), may hold values from 0 to 127, as said below
Outputs:
- attended: bfloat16 [32768, 4096], P(('frames', 'heads'))
- attended_tan: bfloat16 [32768, 4096], P(('frames', 'heads'))
The draws below stay inside these ranges and needn't reach their ends.
Inputs may be any that keep to these rules, and one draw needn't show every extreme that they name: `neighbors`: entry 0 of row b is b itself; the other entries are min(max(b + o, 0), 127) for distinct nonzero offsets o between -4 and 4.
All inputs are finite; a program needn't handle non-finite values.
Results may differ from the reference program's by a relative error of at most 0.028.
Values may be sent and summed in bfloat16 or wider, within the bound.
A program may use at most 192 MiB of HBM per device.

```python
import jax
import jax.numpy as jnp
from jax import lax

HD = 128
HEADS = 32
BQ = 256
WK = 4
HB = 4
TOKENS = 32768
NBLK = 128


def draw_query(key, part):
    key = jax.random.fold_in(key, 1)
    own = jax.random.normal(key, (TOKENS, HEADS * HD), jnp.float32)
    return jnp.clip(own, -6.0, 6.0).astype(jnp.bfloat16)


def draw_keys(key, part):
    key = jax.random.fold_in(key, 2)
    own = jax.random.normal(key, (TOKENS, HEADS * HD), jnp.float32)
    return jnp.clip(own, -6.0, 6.0).astype(jnp.bfloat16)


def draw_neighbors(key, part):
    key = jax.random.fold_in(key, 3)
    ranks = jax.random.randint(key, (NBLK, 2 * HB), 0, 1000, jnp.int32)
    ranks = ranks * (2 * HB) + jnp.arange(2 * HB, dtype=jnp.int32)[None, :]
    order = jnp.argsort(ranks, axis=1, stable=True).astype(jnp.int32)
    offsets = jnp.where(order < HB, order - HB, order - HB + 1)[:, :WK - 1]
    blocks = jnp.arange(NBLK, dtype=jnp.int32)[:, None]
    others = jnp.clip(blocks + offsets, 0, NBLK - 1)
    return jnp.concatenate([blocks, others], axis=1).astype(jnp.int32)


def steps_of(rng, shape, cuts, smallest, largest):
    factor_of = 1.0
    for position, shards_of in cuts:
        draws = jax.random.uniform(jax.random.fold_in(jax.random.fold_in(rng, 6), position), (shards_of,), jnp.float32, smallest / len(cuts), largest / len(cuts))
        factor_of = factor_of * jnp.repeat(jnp.exp(draws), shape[position] // shards_of).reshape((-1,) + (1,) * (len(shape) - 1 - position))
    return factor_of


def bell_draw(stream_key, shape, spread, most, cuts=(), kind=jnp.bfloat16):
    values = jax.random.normal(stream_key, shape, jnp.float32) * spread
    if len(cuts) > 0:
        values = steps_of(stream_key, shape, cuts, -0.22, 0.18) * values
    return jnp.clip(values, min=-most, max=most).astype(kind)


def setup_inputs(seed: int = 0) -> dict:
    key_of = jax.random.split(jax.random.key(seed), 8)
    return {
        "query": draw_query(jax.random.fold_in(key_of[7], 71), 0),
        "keys": draw_keys(jax.random.fold_in(key_of[7], 71), 0),
        "values": bell_draw(key_of[2], (TOKENS, HEADS * HD), 1.0, 6.0, ((0, 256),)),
        "query_tan": bell_draw(key_of[3], (TOKENS, HEADS * HD), 1.0, 6.0, ((0, 256),)),
        "keys_tan": bell_draw(key_of[4], (TOKENS, HEADS * HD), 1.0, 6.0, ((0, 256),)),
        "values_tan": bell_draw(key_of[5], (TOKENS, HEADS * HD), 1.0, 6.0, ((0, 256),)),
        "neighbors": draw_neighbors(jax.random.fold_in(key_of[7], 71), 0),
    }


def one_head(head, query, keys, values, query_tan, keys_tan, values_tan, neighbors):
    start = (head * HD).astype(jnp.int32)

    def cut(array):
        return lax.dynamic_slice_in_dim(array, start, HD, 1)

    def window(array):
        return cut(array).reshape(NBLK, BQ, HD)[neighbors].reshape(NBLK, WK * BQ, HD)

    scale = HD ** -0.5
    q_rows = cut(query).reshape(NBLK, BQ, HD).astype(jnp.float32)
    qt_rows = cut(query_tan).reshape(NBLK, BQ, HD).astype(jnp.float32)
    k_win = window(keys).astype(jnp.float32)
    kt_win = window(keys_tan).astype(jnp.float32)
    v_win = window(values).astype(jnp.float32)
    vt_win = window(values_tan).astype(jnp.float32)
    scores = jnp.einsum("nqd,nkd->nqk", q_rows, k_win) * scale
    probs = jax.nn.softmax(scores, axis=-1)
    probs16 = probs.astype(jnp.bfloat16).astype(jnp.float32)
    out = jnp.einsum("nqk,nkd->nqd", probs16, v_win)
    score_tan = (jnp.einsum("nqd,nkd->nqk", qt_rows, k_win) + jnp.einsum("nqd,nkd->nqk", q_rows, kt_win)) * scale
    weighted = probs * score_tan
    mean_tan = jnp.sum(weighted, axis=-1, keepdims=True)
    weighted16 = weighted.astype(jnp.bfloat16).astype(jnp.float32)
    tan = jnp.einsum("nqk,nkd->nqd", probs16, vt_win) + jnp.einsum("nqk,nkd->nqd", weighted16, v_win) - mean_tan * out
    return out.reshape(TOKENS, HD).astype(jnp.bfloat16), tan.reshape(TOKENS, HD).astype(jnp.bfloat16)


def reference(query, keys, values, query_tan, keys_tan, values_tan, neighbors):
    def step(head):
        return one_head(head, query, keys, values, query_tan, keys_tan, values_tan, neighbors)

    outs, tans = lax.map(step, jnp.arange(HEADS, dtype=jnp.int32))
    attended = jnp.transpose(outs, (1, 0, 2)).reshape(TOKENS, HEADS * HD)
    attended_tan = jnp.transpose(tans, (1, 0, 2)).reshape(TOKENS, HEADS * HD)
    return attended, attended_tan
```

```python
import functools

import jax
import jax.numpy as jnp
from jax import lax
from jax.experimental import pallas as pl
from jax.experimental.pallas import tpu as pltpu
from jax.sharding import PartitionSpec as P

MESH = pl.DeviceIdType.MESH
HD = 128
BQ = 256
WK = 4
HB = 4
HALO = HB * BQ
HEADS = 32
FRAMES = 8
PLANES = 8
TOK = 128
ROWS = HEADS * TOK
PLANE = ROWS // PLANES
BLOCKS = ROWS // BQ
LOG2E = 1.4426950408889634


def partner(me, step):
    turn = lax.rem(step, PLANES)
    half = (turn + 1) // 2
    shift = jnp.where(lax.rem(turn, 2) == 1, PLANES // 2 - half, PLANES // 2 + half)
    plane = lax.rem(me // 4 + shift, PLANES)
    lane = lax.rem(step // PLANES + 1, 4)
    mine = lax.rem(me, 4)
    flip_core = lax.rem(lane, 2)
    flip_x = lane // 2
    core = lax.rem(lax.rem(mine, 2) + flip_core, 2)
    x_lo = lax.rem(mine // 2 + flip_x, 2)
    return plane * 4 + x_lo * 2 + core


def arrived(ref, sem):
    pltpu.make_async_copy(ref, ref, sem).wait()


def kernel(
    nbr, query, keys, values, query_tan, keys_tan, values_tan, out, tan,
    kk, vv, qq, oo, own_sem, send_in, recv_kv, recv_q, send_halo, recv_halo, send_out, recv_out,
):
    me = lax.axis_index("heads")
    frame = lax.axis_index("frames")
    plane = me // 4
    nxt = lax.rem(frame + 1, FRAMES)
    prv = lax.rem(frame + FRAMES - 1, FRAMES)

    barrier = pltpu.get_barrier_semaphore()

    def greet(step, carry):
        pl.semaphore_signal(barrier, inc=1, device_id=(partner(me, step), frame), device_id_type=MESH)
        return carry

    lax.fori_loop(0, HEADS - 1, greet, 0)
    for other in (prv, nxt):
        pl.semaphore_signal(barrier, inc=1, device_id=(me, other), device_id_type=MESH)
    pl.semaphore_wait(barrier, HEADS + 1)

    mine = pl.ds(pl.multiple_of(me * TOK, TOK), TOK)
    mine_kv = pl.ds(pl.multiple_of(HALO + me * TOK, TOK), TOK)
    first, second = pl.ds(0, HD), pl.ds(HD, HD)
    moves = (
        (keys, kk.at[mine_kv, first], recv_kv.at[plane]),
        (values, vv.at[mine_kv, first], recv_kv.at[plane]),
        (keys_tan, kk.at[mine_kv, second], recv_kv.at[plane]),
        (values_tan, vv.at[mine_kv, second], recv_kv.at[plane]),
        (query_tan, qq.at[mine, first], recv_q),
        (query, qq.at[mine, second], recv_q),
    )
    for which, (source, target, sem) in enumerate(moves):

        def send(step, carry, which=which, source=source, target=target, sem=sem):
            head = partner(me, step)
            pltpu.make_async_remote_copy(
                src_ref=source.at[:, pl.ds(pl.multiple_of(head * HD, HD), HD)],
                dst_ref=target,
                send_sem=send_in.at[which],
                recv_sem=sem,
                device_id=(head, frame),
                device_id_type=MESH,
            ).start()
            return carry

        lax.fori_loop(0, HEADS - 1, send, 0)
        pltpu.make_async_copy(
            source.at[:, pl.ds(pl.multiple_of(me * HD, HD), HD)], target, own_sem.at[which]
        ).start()
    for which, (source, target, sem) in enumerate(moves):
        arrived(target, own_sem.at[which])

    def plane_wait(index, skip):
        rows = (HEADS // PLANES - skip) * TOK
        arrived(kk.at[pl.ds(0, 2 * rows), :], recv_kv.at[index])

    def planes_wait(indices):
        for index in indices:

            @pl.when(plane == index)
            def _():
                plane_wait(index, 1)

            @pl.when(plane != index)
            def _():
                plane_wait(index, 0)

    sides = (
        ((0, 1), HALO, HALO + ROWS, prv),
        ((PLANES - 2, PLANES - 1), ROWS, 0, nxt),
    )
    copies = []
    for side, (planes, start, landing, other) in enumerate(sides):
        planes_wait(planes)
        for which, buffer in enumerate((kk, vv)):
            copy = pltpu.make_async_remote_copy(
                src_ref=buffer.at[pl.ds(start, HALO), :],
                dst_ref=buffer.at[pl.ds(landing, HALO), :],
                send_sem=send_halo.at[side, which],
                recv_sem=recv_halo.at[side, which],
                device_id=(me, other),
                device_id_type=MESH,
            )
            copy.start()
            copies.append(copy)
    planes_wait(range(2, PLANES - 2))
    arrived(qq.at[pl.ds(0, ROWS - TOK), :], recv_q)
    for copy in copies:
        copy.wait_recv()

    scale = HD**-0.5
    nt = (((1,), (1,)), ((), ()))
    nn = (((1,), (0,)), ((), ()))

    def block_step(step, carry):
        turn = step // 2
        half = (turn + 1) // 2
        shift = jnp.where(lax.rem(turn, 2) == 1, PLANES // 2 - half, PLANES // 2 + half)
        there = lax.rem(plane + shift, PLANES)
        x_lo = lax.rem(lax.rem(me, 4) // 2 + step + 1, 2)
        block = there * 2 + x_lo
        rows = pl.ds(pl.multiple_of(block * BQ, BQ), BQ)
        both = qq[rows, :]
        q = qq[rows, second]
        wins = []
        for slot in range(WK):
            local = jnp.clip(nbr[block, slot] - frame * BLOCKS + HB, 0, BLOCKS + 2 * HB - 1)
            wins.append(pl.ds(local * BQ, BQ))
        scores = [
            lax.dot_general(q, kk[win, first], nt, preferred_element_type=jnp.float32) for win in wins
        ]
        most = functools.reduce(jnp.maximum, [jnp.max(s, axis=1, keepdims=True) for s in scores])
        total = jnp.zeros((BQ, 1), jnp.float32)
        mean = jnp.zeros((BQ, 1), jnp.float32)
        acc = jnp.zeros((BQ, 2 * HD), jnp.float32)
        acc_w = jnp.zeros((BQ, HD), jnp.float32)
        for s, win in zip(scores, wins):
            p = jnp.exp2((s - most) * (scale * LOG2E))
            st = lax.dot_general(both, kk[win, :], nt, preferred_element_type=jnp.float32)
            w = p * st
            total += jnp.sum(p, axis=1, keepdims=True)
            mean += jnp.sum(w, axis=1, keepdims=True)
            v = vv[win, :]
            acc += lax.dot_general(p.astype(jnp.bfloat16), v, nn, preferred_element_type=jnp.float32)
            acc_w += lax.dot_general(
                w.astype(jnp.bfloat16), v[:, :HD], nn, preferred_element_type=jnp.float32
            )
        inv = 1.0 / total
        o = acc[:, :HD] * inv
        t = (acc[:, HD:] + scale * acc_w) * inv - (scale * mean * inv) * o
        oo[0, rows, :] = o.astype(jnp.bfloat16)
        oo[1, rows, :] = t.astype(jnp.bfloat16)
        column = pl.ds(pl.multiple_of(me * HD, HD), HD)
        core = lax.rem(me, 2)
        for flip in (1, 0):
            there_core = lax.rem(core + flip, 2)
            owner = block * 2 + there_core
            piece = pl.ds(pl.multiple_of(owner * TOK, TOK), TOK)
            for which, result in enumerate((out, tan)):

                def remote(which=which, result=result, owner=owner, piece=piece):
                    pltpu.make_async_remote_copy(
                        src_ref=oo.at[which, piece, :],
                        dst_ref=result.at[:, column],
                        send_sem=send_out.at[which],
                        recv_sem=recv_out.at[which],
                        device_id=(owner, frame),
                        device_id_type=MESH,
                    ).start()

                def local(which=which, result=result, piece=piece):
                    pltpu.make_async_copy(
                        oo.at[which, piece, :], result.at[:, column], own_sem.at[which]
                    ).start()

                if flip:
                    remote()
                else:
                    pl.when(step < BLOCKS - 1)(remote)
                    pl.when(step == BLOCKS - 1)(local)
        return carry

    lax.fori_loop(0, BLOCKS, block_step, 0)

    for copy in copies:
        copy.wait_send()
    for which, (source, target, sem) in enumerate(moves):
        arrived(source.at[:, pl.ds(0, (HEADS - 1) * HD)], send_in.at[which])
    for which, result in enumerate((out, tan)):
        rest = result.at[:, pl.ds(0, (HEADS - 1) * HD)]
        arrived(result.at[:, pl.ds(0, HD)], own_sem.at[which])
        arrived(rest, send_out.at[which])
        arrived(rest, recv_out.at[which])


def per_device(query, keys, values, query_tan, keys_tan, values_tan, neighbors):
    shape = jax.ShapeDtypeStruct((TOK, HEADS * HD), jnp.bfloat16)
    hbm = pl.BlockSpec(memory_space=pl.ANY)
    dma = pltpu.SemaphoreType.DMA
    return pl.pallas_call(
        kernel,
        out_shape=(shape, shape),
        in_specs=[pl.BlockSpec(memory_space=pltpu.SMEM)] + [hbm] * 6,
        out_specs=(hbm, hbm),
        scratch_shapes=[
            pltpu.VMEM((ROWS + 2 * HALO, 2 * HD), jnp.bfloat16),
            pltpu.VMEM((ROWS + 2 * HALO, 2 * HD), jnp.bfloat16),
            pltpu.VMEM((ROWS, 2 * HD), jnp.bfloat16),
            pltpu.VMEM((2, ROWS, HD), jnp.bfloat16),
            dma((6,)),
            dma((6,)),
            dma((PLANES,)),
            dma,
            dma((2, 2)),
            dma((2, 2)),
            dma((2,)),
            dma((2,)),
        ],
        compiler_params=pltpu.CompilerParams(
            collective_id=0, has_side_effects=True, vmem_limit_bytes=56 << 20
        ),
        cost_estimate=pl.CostEstimate(
            flops=7 * 10**9, bytes_accessed=20 << 20, transcendentals=5 * 10**6
        ),
        name="attend",
    )(neighbors, query, keys, values, query_tan, keys_tan, values_tan)


def solution(mesh):
    tokens = P(("frames", "heads"), None)
    return jax.shard_map(
        per_device,
        mesh=mesh,
        in_specs=(tokens,) * 6 + (P("frames", None),),
        out_specs=(tokens, tokens),
        check_vma=False,
    )
```

```python
import functools

import jax
import jax.numpy as jnp
from jax import lax
from jax.experimental import pallas as pl
from jax.experimental.pallas import tpu as pltpu
from jax.sharding import PartitionSpec as P

MESH = pl.DeviceIdType.MESH
HD = 128
BQ = 256
WK = 4
HB = 4
HALO = HB * BQ
HEADS = 32
FRAMES = 8
PLANES = 8
TOK = 128
ROWS = HEADS * TOK
PLANE = ROWS // PLANES
BLOCKS = ROWS // BQ
LOG2E = 1.4426950408889634


def partner(me, step):
    turn = lax.rem(step, PLANES)
    half = (turn + 1) // 2
    shift = jnp.where(lax.rem(turn, 2) == 1, PLANES // 2 - half, PLANES // 2 + half)
    plane = lax.rem(me // 4 + shift, PLANES)
    lane = lax.rem(step // PLANES + 1, 4)
    mine = lax.rem(me, 4)
    flip_core = lax.rem(lane, 2)
    flip_x = lane // 2
    core = lax.rem(lax.rem(mine, 2) + flip_core, 2)
    x_lo = lax.rem(mine // 2 + flip_x, 2)
    return plane * 4 + x_lo * 2 + core


def head_of(device, frame):
    x_lo = lax.rem(device // 2, 2)
    return device + 2 * lax.rem(frame, 2) * (1 - 2 * x_lo)


def arrived(ref, sem):
    pltpu.make_async_copy(ref, ref, sem).wait()


def kernel(
    nbr, query, keys, values, query_tan, keys_tan, values_tan, out, tan,
    kk, vv, qq, oo, send_in, recv_kv, recv_q, send_halo, recv_halo, send_out, recv_out,
):
    me = lax.axis_index("heads")
    frame = lax.axis_index("frames")
    plane = me // 4
    nxt = lax.rem(frame + 1, FRAMES)
    prv = lax.rem(frame + FRAMES - 1, FRAMES)
    beside = me + 2 * (1 - 2 * lax.rem(me // 2, 2))

    barrier = pltpu.get_barrier_semaphore()

    def greet(step, carry):
        pl.semaphore_signal(barrier, inc=1, device_id=(partner(me, step), frame), device_id_type=MESH)
        return carry

    lax.fori_loop(0, HEADS - 1, greet, 0)
    for other in (prv, nxt):
        pl.semaphore_signal(barrier, inc=1, device_id=(beside, other), device_id_type=MESH)
    pl.semaphore_wait(barrier, HEADS + 1)

    mine = pl.ds(pl.multiple_of(me * TOK, TOK), TOK)
    mine_kv = pl.ds(pl.multiple_of(HALO + me * TOK, TOK), TOK)
    first, second = pl.ds(0, HD), pl.ds(HD, HD)
    group = (plane + 2) // 4
    window = ((keys, kk, first), (values, vv, first), (keys_tan, kk, second), (values_tan, vv, second))
    queries = ((query_tan, first), (query, second))

    def column(device):
        return pl.ds(pl.multiple_of(head_of(device, frame) * HD, HD), HD)

    def send_window(which):
        source, buffer, part = window[which]
        target, sem = buffer.at[mine_kv, part], recv_kv.at[which, group]

        def send(step, carry):
            there = partner(me, step)
            pltpu.make_async_remote_copy(
                src_ref=source.at[:, column(there)],
                dst_ref=target,
                send_sem=send_in.at[which],
                recv_sem=sem,
                device_id=(there, frame),
                device_id_type=MESH,
            ).start()
            return carry

        lax.fori_loop(0, HEADS - 1, send, 0)
        pltpu.make_async_copy(source.at[:, column(me)], target, sem).start()

    def send_queries(start, stop):
        def send(step, carry):
            there = partner(me, lax.rem(step, 4) * PLANES + step // 4)
            for which, (source, part) in enumerate(queries):
                pltpu.make_async_remote_copy(
                    src_ref=source.at[:, column(there)],
                    dst_ref=qq.at[mine, part],
                    send_sem=send_in.at[4 + which],
                    recv_sem=recv_q.at[plane],
                    device_id=(there, frame),
                    device_id_type=MESH,
                ).start()
            return carry

        lax.fori_loop(start, stop, send, 0)

    copies = []

    def forward(which):
        buffer, part = window[which][1:]
        sides = ((0, HALO, HALO + ROWS, prv), (2, ROWS, 0, nxt))
        for side, (edge, start, landing, other) in enumerate(sides):
            arrived(buffer.at[pl.ds(start, HALO), part], recv_kv.at[which, edge])
            copy = pltpu.make_async_remote_copy(
                src_ref=buffer.at[pl.ds(start, HALO), part],
                dst_ref=buffer.at[pl.ds(landing, HALO), part],
                send_sem=send_halo.at[which, side],
                recv_sem=recv_halo.at[which, side],
                device_id=(beside, other),
                device_id_type=MESH,
            )
            copy.start()
            copies.append(copy)

    send_window(0)
    send_window(1)
    forward(0)
    send_window(2)
    forward(1)
    send_window(3)
    forward(2)
    send_queries(0, 12)
    forward(3)
    send_queries(12, HEADS - 1)
    for which, (source, part) in enumerate(queries):
        pltpu.make_async_copy(source.at[:, column(me)], qq.at[mine, part], recv_q.at[plane]).start()
    for which, (source, buffer, part) in enumerate(window):
        arrived(buffer.at[pl.ds(HALO + 2 * PLANE, 4 * PLANE), part], recv_kv.at[which, 1])
    for copy in copies:
        copy.wait_recv()

    scale = HD**-0.5
    nt = (((1,), (1,)), ((), ()))
    nn = (((1,), (0,)), ((), ()))

    def block_step(step, carry):
        turn = step // 2
        half = (turn + 1) // 2
        shift = jnp.where(lax.rem(turn, 2) == 1, PLANES // 2 - half, PLANES // 2 + half)
        there = lax.rem(plane + shift, PLANES)
        x_lo = lax.rem(lax.rem(me, 4) // 2 + step + 1, 2)
        block = there * 2 + x_lo
        rows = pl.ds(pl.multiple_of(block * BQ, BQ), BQ)

        @pl.when(lax.rem(step, 2) == 0)
        def _():
            arrived(qq.at[pl.ds(pl.multiple_of(there * PLANE, PLANE), PLANE), :], recv_q.at[there])

        both = qq[rows, :]
        q = qq[rows, second]
        wins = []
        for slot in range(WK):
            local = jnp.clip(nbr[slot, block] - frame * BLOCKS + HB, 0, BLOCKS + 2 * HB - 1)
            wins.append(pl.ds(local * BQ, BQ))
        scores = [
            lax.dot_general(q, kk[win, first], nt, preferred_element_type=jnp.float32) for win in wins
        ]
        most = functools.reduce(jnp.maximum, [jnp.max(s, axis=1, keepdims=True) for s in scores])
        total = jnp.zeros((BQ, 1), jnp.float32)
        mean = jnp.zeros((BQ, 1), jnp.float32)
        acc = jnp.zeros((BQ, 2 * HD), jnp.float32)
        acc_w = jnp.zeros((BQ, HD), jnp.float32)
        for s, win in zip(scores, wins):
            p = jnp.exp2((s - most) * (scale * LOG2E))
            st = lax.dot_general(both, kk[win, :], nt, preferred_element_type=jnp.float32)
            w = p * st
            total += jnp.sum(p, axis=1, keepdims=True)
            mean += jnp.sum(w, axis=1, keepdims=True)
            v = vv[win, :]
            acc += lax.dot_general(p.astype(jnp.bfloat16), v, nn, preferred_element_type=jnp.float32)
            acc_w += lax.dot_general(
                w.astype(jnp.bfloat16), v[:, :HD], nn, preferred_element_type=jnp.float32
            )
        inv = 1.0 / total
        o = acc[:, :HD] * inv
        t = (acc[:, HD:] + scale * acc_w) * inv - (scale * mean * inv) * o
        oo[0, rows, :] = o.astype(jnp.bfloat16)
        oo[1, rows, :] = t.astype(jnp.bfloat16)
        home = column(me)
        core = lax.rem(me, 2)
        for flip in (1, 0):
            there_core = lax.rem(core + flip, 2)
            owner = block * 2 + there_core
            piece = pl.ds(pl.multiple_of(owner * TOK, TOK), TOK)
            for which, result in enumerate((out, tan)):

                def remote(which=which, result=result, owner=owner, piece=piece):
                    pltpu.make_async_remote_copy(
                        src_ref=oo.at[which, piece, :],
                        dst_ref=result.at[:, home],
                        send_sem=send_out.at[which],
                        recv_sem=recv_out.at[which],
                        device_id=(owner, frame),
                        device_id_type=MESH,
                    ).start()

                def local(which=which, result=result, piece=piece):
                    pltpu.make_async_copy(
                        oo.at[which, piece, :], result.at[:, home], recv_out.at[which]
                    ).start()

                if flip:
                    remote()
                else:
                    pl.when(step < BLOCKS - 1)(remote)
                    pl.when(step == BLOCKS - 1)(local)
        return carry

    lax.fori_loop(0, BLOCKS, block_step, 0)

    for copy in copies:
        copy.wait_send()
    rest = pl.ds(0, (HEADS - 1) * HD)
    for which in range(6):
        arrived(out.at[:, rest], send_in.at[which])
    for which, result in enumerate((out, tan)):
        arrived(result.at[:, rest], send_out.at[which])
        arrived(result, recv_out.at[which])


def per_device(query, keys, values, query_tan, keys_tan, values_tan, neighbors):
    shape = jax.ShapeDtypeStruct((TOK, HEADS * HD), jnp.bfloat16)
    hbm = pl.BlockSpec(memory_space=pl.ANY)
    dma = pltpu.SemaphoreType.DMA
    return pl.pallas_call(
        kernel,
        out_shape=(shape, shape),
        in_specs=[pl.BlockSpec(memory_space=pltpu.SMEM)] + [hbm] * 6,
        out_specs=(hbm, hbm),
        scratch_shapes=[
            pltpu.VMEM((ROWS + 2 * HALO, 2 * HD), jnp.bfloat16),
            pltpu.VMEM((ROWS + 2 * HALO, 2 * HD), jnp.bfloat16),
            pltpu.VMEM((ROWS, 2 * HD), jnp.bfloat16),
            pltpu.VMEM((2, ROWS, HD), jnp.bfloat16),
            dma((6,)),
            dma((4, 3)),
            dma((PLANES,)),
            dma((4, 2)),
            dma((4, 2)),
            dma((2,)),
            dma((2,)),
        ],
        compiler_params=pltpu.CompilerParams(
            collective_id=0, has_side_effects=True, vmem_limit_bytes=56 << 20
        ),
        cost_estimate=pl.CostEstimate(
            flops=7 * 10**9, bytes_accessed=20 << 20, transcendentals=5 * 10**6
        ),
        name="attend",
    )(neighbors.T, query, keys, values, query_tan, keys_tan, values_tan)


def solution(mesh):
    tokens = P(("frames", "heads"), None)
    return jax.shard_map(
        per_device,
        mesh=mesh,
        in_specs=(tokens,) * 6 + (P("frames", None),),
        out_specs=(tokens, tokens),
        check_vma=False,
    )
```

```python
import functools

import jax
import jax.numpy as jnp
from jax import lax
from jax.experimental import pallas as pl
from jax.experimental.pallas import tpu as pltpu
from jax.sharding import PartitionSpec as P

MESH = pl.DeviceIdType.MESH
HD = 128
BQ = 256
WK = 4
HB = 4
HALO = HB * BQ
HEADS = 32
FRAMES = 8
PLANES = 8
TOK = 128
ROWS = HEADS * TOK
PLANE = ROWS // PLANES
BLOCKS = ROWS // BQ
LOG2E = 1.4426950408889634


def partner(me, step):
    turn = lax.rem(step, PLANES)
    half = (turn + 1) // 2
    shift = jnp.where(lax.rem(turn, 2) == 1, PLANES // 2 - half, PLANES // 2 + half)
    plane = lax.rem(me // 4 + shift, PLANES)
    lane = lax.rem(step // PLANES + 1, 4)
    mine = lax.rem(me, 4)
    flip_core = lax.rem(lane, 2)
    flip_x = lane // 2
    core = lax.rem(lax.rem(mine, 2) + flip_core, 2)
    x_lo = lax.rem(mine // 2 + flip_x, 2)
    return plane * 4 + x_lo * 2 + core


def head_of(device, frame):
    x_lo = lax.rem(device // 2, 2)
    return device + 2 * lax.rem(frame, 2) * (1 - 2 * x_lo)


def arrived(ref, sem):
    pltpu.make_async_copy(ref, ref, sem).wait()


def kernel(
    nbr, query, keys, values, query_tan, keys_tan, values_tan, out, tan,
    kk, vv, qq, oo, send_in, recv_kv, recv_q, send_halo, recv_halo, send_out, recv_out,
):
    me = lax.axis_index("heads")
    frame = lax.axis_index("frames")
    plane = me // 4
    nxt = lax.rem(frame + 1, FRAMES)
    prv = lax.rem(frame + FRAMES - 1, FRAMES)
    beside = me + 2 * (1 - 2 * lax.rem(me // 2, 2))

    barrier = pltpu.get_barrier_semaphore()

    mates = [lax.rem(me, 4), beside - 4 * plane]
    mates = mates + [mate + 1 - 2 * lax.rem(mate, 2) for mate in mates]
    for shift in (4, 3, 5, 2, 6, 1, 7, 0):
        there = lax.rem(plane + shift, PLANES) * 4
        for mate in mates[1:] if shift == 0 else mates:
            pl.semaphore_signal(barrier, inc=1, device_id=(there + mate, frame), device_id_type=MESH)
    for other in (prv, nxt):
        pl.semaphore_signal(barrier, inc=1, device_id=(beside, other), device_id_type=MESH)
    pl.semaphore_wait(barrier, HEADS + 1)

    mine = pl.ds(pl.multiple_of(me * TOK, TOK), TOK)
    mine_kv = pl.ds(pl.multiple_of(HALO + me * TOK, TOK), TOK)
    first, second = pl.ds(0, HD), pl.ds(HD, HD)
    group = (plane + 2) // 4
    window = ((keys, kk, first), (values, vv, first), (keys_tan, kk, second), (values_tan, vv, second))
    queries = ((query_tan, first), (query, second))

    def column(device):
        return pl.ds(pl.multiple_of(head_of(device, frame) * HD, HD), HD)

    def send_window(which):
        source, buffer, part = window[which]
        target, sem = buffer.at[mine_kv, part], recv_kv.at[which, group]

        def send(step, carry):
            there = partner(me, step)
            pltpu.make_async_remote_copy(
                src_ref=source.at[:, column(there)],
                dst_ref=target,
                send_sem=send_in.at[which],
                recv_sem=sem,
                device_id=(there, frame),
                device_id_type=MESH,
            ).start()
            return carry

        lax.fori_loop(0, HEADS - 1, send, 0)
        pltpu.make_async_copy(source.at[:, column(me)], target, sem).start()

    def send_queries(start, stop):
        def send(step, carry):
            there = partner(me, lax.rem(step, 4) * PLANES + step // 4)
            for which, (source, part) in enumerate(queries):
                pltpu.make_async_remote_copy(
                    src_ref=source.at[:, column(there)],
                    dst_ref=qq.at[mine, part],
                    send_sem=send_in.at[4 + which],
                    recv_sem=recv_q.at[plane],
                    device_id=(there, frame),
                    device_id_type=MESH,
                ).start()
            return carry

        lax.fori_loop(start, stop, send, 0)

    copies = []

    def forward(which):
        buffer, part = window[which][1:]
        sides = ((0, HALO, HALO + ROWS, prv), (2, ROWS, 0, nxt))
        for side, (edge, start, landing, other) in enumerate(sides):
            arrived(buffer.at[pl.ds(start, HALO), part], recv_kv.at[which, edge])
            copy = pltpu.make_async_remote_copy(
                src_ref=buffer.at[pl.ds(start, HALO), part],
                dst_ref=buffer.at[pl.ds(landing, HALO), part],
                send_sem=send_halo.at[which, side],
                recv_sem=recv_halo.at[which, side],
                device_id=(beside, other),
                device_id_type=MESH,
            )
            copy.start()
            copies.append(copy)

    send_window(0)
    send_window(1)
    forward(0)
    send_window(2)
    forward(1)
    send_window(3)
    forward(2)
    send_queries(0, 12)
    forward(3)
    send_queries(12, HEADS - 1)
    for which, (source, part) in enumerate(queries):
        pltpu.make_async_copy(source.at[:, column(me)], qq.at[mine, part], recv_q.at[plane]).start()
    for which, (source, buffer, part) in enumerate(window):
        arrived(buffer.at[pl.ds(HALO + 2 * PLANE, 4 * PLANE), part], recv_kv.at[which, 1])
    for copy in copies:
        copy.wait_recv()

    scale = HD**-0.5
    nt = (((1,), (1,)), ((), ()))
    nn = (((1,), (0,)), ((), ()))

    def block_step(step, carry):
        turn = step // 2
        half = (turn + 1) // 2
        shift = jnp.where(lax.rem(turn, 2) == 1, PLANES // 2 - half, PLANES // 2 + half)
        there = lax.rem(plane + shift, PLANES)
        x_lo = lax.rem(lax.rem(me, 4) // 2 + step + 1, 2)
        block = there * 2 + x_lo
        rows = pl.ds(pl.multiple_of(block * BQ, BQ), BQ)

        @pl.when(lax.rem(step, 2) == 0)
        def _():
            arrived(qq.at[pl.ds(pl.multiple_of(there * PLANE, PLANE), PLANE), :], recv_q.at[there])

        both = qq[rows, :]
        q = qq[rows, second]
        wins = []
        for slot in range(WK):
            local = jnp.clip(nbr[slot, block] - frame * BLOCKS + HB, 0, BLOCKS + 2 * HB - 1)
            wins.append(pl.ds(local * BQ, BQ))
        scores = [
            lax.dot_general(q, kk[win, first], nt, preferred_element_type=jnp.float32) for win in wins
        ]
        most = functools.reduce(jnp.maximum, [jnp.max(s, axis=1, keepdims=True) for s in scores])
        total = jnp.zeros((BQ, 1), jnp.float32)
        mean = jnp.zeros((BQ, 1), jnp.float32)
        acc = jnp.zeros((BQ, 2 * HD), jnp.float32)
        acc_w = jnp.zeros((BQ, HD), jnp.float32)
        for s, win in zip(scores, wins):
            p = jnp.exp2((s - most) * (scale * LOG2E))
            st = lax.dot_general(both, kk[win, :], nt, preferred_element_type=jnp.float32)
            w = p * st
            total += jnp.sum(p, axis=1, keepdims=True)
            mean += jnp.sum(w, axis=1, keepdims=True)
            v = vv[win, :]
            acc += lax.dot_general(p.astype(jnp.bfloat16), v, nn, preferred_element_type=jnp.float32)
            acc_w += lax.dot_general(
                w.astype(jnp.bfloat16), v[:, :HD], nn, preferred_element_type=jnp.float32
            )
        inv = 1.0 / total
        o = acc[:, :HD] * inv
        t = (acc[:, HD:] + scale * acc_w) * inv - (scale * mean * inv) * o
        oo[0, rows, :] = o.astype(jnp.bfloat16)
        oo[1, rows, :] = t.astype(jnp.bfloat16)
        home = column(me)
        core = lax.rem(me, 2)
        for flip in (1, 0):
            there_core = lax.rem(core + flip, 2)
            owner = block * 2 + there_core
            piece = pl.ds(pl.multiple_of(owner * TOK, TOK), TOK)
            for which, result in enumerate((out, tan)):

                def remote(which=which, result=result, owner=owner, piece=piece):
                    pltpu.make_async_remote_copy(
                        src_ref=oo.at[which, piece, :],
                        dst_ref=result.at[:, home],
                        send_sem=send_out.at[which],
                        recv_sem=recv_out.at[which],
                        device_id=(owner, frame),
                        device_id_type=MESH,
                    ).start()

                def local(which=which, result=result, piece=piece):
                    pltpu.make_async_copy(
                        oo.at[which, piece, :], result.at[:, home], recv_out.at[which]
                    ).start()

                if flip:
                    remote()
                else:
                    pl.when(step < BLOCKS - 1)(remote)
                    pl.when(step == BLOCKS - 1)(local)
        return carry

    lax.fori_loop(0, BLOCKS, block_step, 0)

    for copy in copies:
        copy.wait_send()
    rest = pl.ds(0, (HEADS - 1) * HD)
    for which in range(6):
        arrived(out.at[:, rest], send_in.at[which])
    for which, result in enumerate((out, tan)):
        arrived(result.at[:, rest], send_out.at[which])
        arrived(result, recv_out.at[which])


def per_device(query, keys, values, query_tan, keys_tan, values_tan, neighbors):
    shape = jax.ShapeDtypeStruct((TOK, HEADS * HD), jnp.bfloat16)
    hbm = pl.BlockSpec(memory_space=pl.ANY)
    dma = pltpu.SemaphoreType.DMA
    return pl.pallas_call(
        kernel,
        out_shape=(pltpu.VMEM((TOK, HEADS * HD), jnp.bfloat16),) * 2,
        in_specs=[pl.BlockSpec(memory_space=pltpu.SMEM)] + [hbm] * 6,
        out_specs=(hbm, hbm),
        scratch_shapes=[
            pltpu.VMEM((ROWS + 2 * HALO, 2 * HD), jnp.bfloat16),
            pltpu.VMEM((ROWS + 2 * HALO, 2 * HD), jnp.bfloat16),
            pltpu.VMEM((ROWS, 2 * HD), jnp.bfloat16),
            pltpu.VMEM((2, ROWS, HD), jnp.bfloat16),
            dma((6,)),
            dma((4, 3)),
            dma((PLANES,)),
            dma((4, 2)),
            dma((4, 2)),
            dma((2,)),
            dma((2,)),
        ],
        compiler_params=pltpu.CompilerParams(
            collective_id=0, has_side_effects=True, vmem_limit_bytes=56 << 20
        ),
        cost_estimate=pl.CostEstimate(
            flops=7 * 10**9, bytes_accessed=20 << 20, transcendentals=5 * 10**6
        ),
        name="attend",
    )(neighbors.T, query, keys, values, query_tan, keys_tan, values_tan)


def solution(mesh):
    tokens = P(("frames", "heads"), None)
    return jax.shard_map(
        per_device,
        mesh=mesh,
        in_specs=(tokens,) * 6 + (P("frames", None),),
        out_specs=(tokens, tokens),
        check_vma=False,
    )
```

```python
import functools

import jax
import jax.numpy as jnp
from jax import lax
from jax.experimental import pallas as pl
from jax.experimental.pallas import tpu as pltpu
from jax.sharding import PartitionSpec as P

MESH = pl.DeviceIdType.MESH
HD = 128
BQ = 256
WK = 4
HB = 4
HALO = HB * BQ
HEADS = 32
FRAMES = 8
PLANES = 8
TOK = 128
ROWS = HEADS * TOK
PLANE = ROWS // PLANES
BLOCKS = ROWS // BQ
LOG2E = 1.4426950408889634


def partner(me, step):
    turn = lax.rem(step, PLANES)
    half = (turn + 1) // 2
    shift = jnp.where(lax.rem(turn, 2) == 1, PLANES // 2 - half, PLANES // 2 + half)
    plane = lax.rem(me // 4 + shift, PLANES)
    lane = lax.rem(step // PLANES + 1, 4)
    mine = lax.rem(me, 4)
    flip_core = lax.rem(lane, 2)
    flip_x = lane // 2
    core = lax.rem(lax.rem(mine, 2) + flip_core, 2)
    x_lo = lax.rem(mine // 2 + flip_x, 2)
    return plane * 4 + x_lo * 2 + core


def head_of(device, frame):
    x_lo = lax.rem(device // 2, 2)
    return device + 2 * lax.rem(frame, 2) * (1 - 2 * x_lo)


def arrived(ref, sem):
    pltpu.make_async_copy(ref, ref, sem).wait()


def kernel(
    table, query, keys, values, query_tan, keys_tan, values_tan, out, tan,
    nbr, kk, vv, qq, oo, table_sem, send_in, recv_kv, recv_q, send_halo, recv_halo, send_out, recv_out,
):
    me = lax.axis_index("heads")
    frame = lax.axis_index("frames")
    plane = me // 4
    nxt = lax.rem(frame + 1, FRAMES)
    prv = lax.rem(frame + FRAMES - 1, FRAMES)
    beside = me + 2 * (1 - 2 * lax.rem(me // 2, 2))

    barrier = pltpu.get_barrier_semaphore()

    mates = [lax.rem(me, 4), beside - 4 * plane]
    mates = mates + [mate + 1 - 2 * lax.rem(mate, 2) for mate in mates]
    for shift in (4, 3, 5, 2, 6, 1, 7, 0):
        there = lax.rem(plane + shift, PLANES) * 4
        for mate in mates[1:] if shift == 0 else mates:
            pl.semaphore_signal(barrier, inc=1, device_id=(there + mate, frame), device_id_type=MESH)
    for other in (prv, nxt):
        pl.semaphore_signal(barrier, inc=1, device_id=(beside, other), device_id_type=MESH)
    fetch = pltpu.make_async_copy(table, nbr, table_sem)
    fetch.start()
    pl.semaphore_wait(barrier, HEADS + 1)

    mine = pl.ds(pl.multiple_of(me * TOK, TOK), TOK)
    mine_kv = pl.ds(pl.multiple_of(HALO + me * TOK, TOK), TOK)
    first, second = pl.ds(0, HD), pl.ds(HD, HD)
    group = (plane + 2) // 4
    window = ((keys, kk, first), (values, vv, first), (keys_tan, kk, second), (values_tan, vv, second))
    queries = ((query_tan, first), (query, second))

    def column(device):
        return pl.ds(pl.multiple_of(head_of(device, frame) * HD, HD), HD)

    def send_window(which):
        source, buffer, part = window[which]
        target, sem = buffer.at[mine_kv, part], recv_kv.at[which, group]

        def send(step, carry):
            there = partner(me, step)
            pltpu.make_async_remote_copy(
                src_ref=source.at[:, column(there)],
                dst_ref=target,
                send_sem=send_in.at[which],
                recv_sem=sem,
                device_id=(there, frame),
                device_id_type=MESH,
            ).start()
            return carry

        lax.fori_loop(0, HEADS - 1, send, 0)
        pltpu.make_async_copy(source.at[:, column(me)], target, sem).start()

    def send_queries(start, stop):
        def send(step, carry):
            there = partner(me, lax.rem(step, 4) * PLANES + step // 4)
            for which, (source, part) in enumerate(queries):
                pltpu.make_async_remote_copy(
                    src_ref=source.at[:, column(there)],
                    dst_ref=qq.at[mine, part],
                    send_sem=send_in.at[4 + which],
                    recv_sem=recv_q.at[plane],
                    device_id=(there, frame),
                    device_id_type=MESH,
                ).start()
            return carry

        lax.fori_loop(start, stop, send, 0)

    copies = []

    def forward(which):
        buffer, part = window[which][1:]
        sides = ((0, HALO, HALO + ROWS, prv), (2, ROWS, 0, nxt))
        for side, (edge, start, landing, other) in enumerate(sides):
            arrived(buffer.at[pl.ds(start, HALO), part], recv_kv.at[which, edge])
            copy = pltpu.make_async_remote_copy(
                src_ref=buffer.at[pl.ds(start, HALO), part],
                dst_ref=buffer.at[pl.ds(landing, HALO), part],
                send_sem=send_halo.at[which, side],
                recv_sem=recv_halo.at[which, side],
                device_id=(beside, other),
                device_id_type=MESH,
            )
            copy.start()
            copies.append(copy)

    send_window(0)
    send_window(1)
    forward(0)
    send_window(2)
    forward(1)
    send_window(3)
    forward(2)
    send_queries(0, 12)
    forward(3)
    send_queries(12, HEADS - 1)
    for which, (source, part) in enumerate(queries):
        pltpu.make_async_copy(source.at[:, column(me)], qq.at[mine, part], recv_q.at[plane]).start()
    for which, (source, buffer, part) in enumerate(window):
        arrived(buffer.at[pl.ds(HALO + 2 * PLANE, 4 * PLANE), part], recv_kv.at[which, 1])
    for copy in copies:
        copy.wait_recv()
    fetch.wait()

    scale = HD**-0.5
    nt = (((1,), (1,)), ((), ()))
    nn = (((1,), (0,)), ((), ()))

    def block_step(step, carry):
        turn = step // 2
        half = (turn + 1) // 2
        shift = jnp.where(lax.rem(turn, 2) == 1, PLANES // 2 - half, PLANES // 2 + half)
        there = lax.rem(plane + shift, PLANES)
        x_lo = lax.rem(lax.rem(me, 4) // 2 + step + 1, 2)
        block = there * 2 + x_lo
        rows = pl.ds(pl.multiple_of(block * BQ, BQ), BQ)

        @pl.when(lax.rem(step, 2) == 0)
        def _():
            arrived(qq.at[pl.ds(pl.multiple_of(there * PLANE, PLANE), PLANE), :], recv_q.at[there])

        both = qq[rows, :]
        q = qq[rows, second]
        wins = []
        for slot in range(WK):
            local = jnp.clip(nbr[slot, block] - frame * BLOCKS + HB, 0, BLOCKS + 2 * HB - 1)
            wins.append(pl.ds(local * BQ, BQ))
        scores = [
            lax.dot_general(q, kk[win, first], nt, preferred_element_type=jnp.float32) for win in wins
        ]
        most = functools.reduce(jnp.maximum, [jnp.max(s, axis=1, keepdims=True) for s in scores])
        total = jnp.zeros((BQ, 1), jnp.float32)
        mean = jnp.zeros((BQ, 1), jnp.float32)
        acc = jnp.zeros((BQ, 2 * HD), jnp.float32)
        acc_w = jnp.zeros((BQ, HD), jnp.float32)
        for s, win in zip(scores, wins):
            p = jnp.exp2((s - most) * (scale * LOG2E))
            st = lax.dot_general(both, kk[win, :], nt, preferred_element_type=jnp.float32)
            w = p * st
            total += jnp.sum(p, axis=1, keepdims=True)
            mean += jnp.sum(w, axis=1, keepdims=True)
            v = vv[win, :]
            acc += lax.dot_general(p.astype(jnp.bfloat16), v, nn, preferred_element_type=jnp.float32)
            acc_w += lax.dot_general(
                w.astype(jnp.bfloat16), v[:, :HD], nn, preferred_element_type=jnp.float32
            )
        inv = 1.0 / total
        o = acc[:, :HD] * inv
        t = (acc[:, HD:] + scale * acc_w) * inv - (scale * mean * inv) * o
        oo[0, rows, :] = o.astype(jnp.bfloat16)
        oo[1, rows, :] = t.astype(jnp.bfloat16)
        home = column(me)
        core = lax.rem(me, 2)
        for flip in (1, 0):
            there_core = lax.rem(core + flip, 2)
            owner = block * 2 + there_core
            piece = pl.ds(pl.multiple_of(owner * TOK, TOK), TOK)
            for which, result in enumerate((out, tan)):

                def remote(which=which, result=result, owner=owner, piece=piece):
                    pltpu.make_async_remote_copy(
                        src_ref=oo.at[which, piece, :],
                        dst_ref=result.at[:, home],
                        send_sem=send_out.at[which],
                        recv_sem=recv_out.at[which],
                        device_id=(owner, frame),
                        device_id_type=MESH,
                    ).start()

                def local(which=which, result=result, piece=piece):
                    pltpu.make_async_copy(
                        oo.at[which, piece, :], result.at[:, home], recv_out.at[which]
                    ).start()

                if flip:
                    remote()
                else:
                    pl.when(step < BLOCKS - 1)(remote)
                    pl.when(step == BLOCKS - 1)(local)
        return carry

    lax.fori_loop(0, BLOCKS, block_step, 0)

    for copy in copies:
        copy.wait_send()
    rest = pl.ds(0, (HEADS - 1) * HD)
    for which in range(6):
        arrived(out.at[:, rest], send_in.at[which])
    for which, result in enumerate((out, tan)):
        arrived(result.at[:, rest], send_out.at[which])
        arrived(result, recv_out.at[which])


def per_device(query, keys, values, query_tan, keys_tan, values_tan, neighbors):
    shape = jax.ShapeDtypeStruct((TOK, HEADS * HD), jnp.bfloat16)
    hbm = pl.BlockSpec(memory_space=pl.ANY)
    dma = pltpu.SemaphoreType.DMA
    return pl.pallas_call(
        kernel,
        out_shape=(pltpu.VMEM((TOK, HEADS * HD), jnp.bfloat16),) * 2,
        in_specs=[hbm] * 7,
        out_specs=(hbm, hbm),
        scratch_shapes=[
            pltpu.SMEM((WK, BLOCKS), jnp.int32),
            pltpu.VMEM((ROWS + 2 * HALO, 2 * HD), jnp.bfloat16),
            pltpu.VMEM((ROWS + 2 * HALO, 2 * HD), jnp.bfloat16),
            pltpu.VMEM((ROWS, 2 * HD), jnp.bfloat16),
            pltpu.VMEM((2, ROWS, HD), jnp.bfloat16),
            dma,
            dma((6,)),
            dma((4, 3)),
            dma((PLANES,)),
            dma((4, 2)),
            dma((4, 2)),
            dma((2,)),
            dma((2,)),
        ],
        compiler_params=pltpu.CompilerParams(
            collective_id=0, has_side_effects=True, vmem_limit_bytes=56 << 20
        ),
        cost_estimate=pl.CostEstimate(
            flops=7 * 10**9, bytes_accessed=20 << 20, transcendentals=5 * 10**6
        ),
        name="attend",
    )(neighbors.T, query, keys, values, query_tan, keys_tan, values_tan)


def solution(mesh):
    tokens = P(("frames", "heads"), None)
    return jax.shard_map(
        per_device,
        mesh=mesh,
        in_specs=(tokens,) * 6 + (P("frames", None),),
        out_specs=(tokens, tokens),
        check_vma=False,
    )
```

```python
import functools

import jax
import jax.numpy as jnp
from jax import lax
from jax.experimental import pallas as pl
from jax.experimental.pallas import tpu as pltpu
from jax.sharding import PartitionSpec as P

MESH = pl.DeviceIdType.MESH
HD = 128
BQ = 256
WK = 4
HB = 4
HALO = HB * BQ
HEADS = 32
FRAMES = 8
PLANES = 8
TOK = 128
ROWS = HEADS * TOK
PLANE = ROWS // PLANES
BLOCKS = ROWS // BQ
LOG2E = 1.4426950408889634


def partner(me, step):
    turn = lax.rem(step, PLANES)
    half = (turn + 1) // 2
    shift = jnp.where(lax.rem(turn, 2) == 1, PLANES // 2 - half, PLANES // 2 + half)
    plane = lax.rem(me // 4 + shift, PLANES)
    lane = lax.rem(step // PLANES + 1, 4)
    mine = lax.rem(me, 4)
    flip_core = lax.rem(lane, 2)
    flip_x = lane // 2
    core = lax.rem(lax.rem(mine, 2) + flip_core, 2)
    x_lo = lax.rem(mine // 2 + flip_x, 2)
    return plane * 4 + x_lo * 2 + core


def head_of(device, frame):
    x_lo = lax.rem(device // 2, 2)
    return device + 2 * lax.rem(frame, 2) * (1 - 2 * x_lo)


def arrived(ref, sem):
    pltpu.make_async_copy(ref, ref, sem).wait()


def kernel(
    table, query, keys, values, query_tan, keys_tan, values_tan, out, tan,
    nbr, kk, vv, qq, oo, ready, table_sem, send_in, recv_kv, recv_q, send_halo, recv_halo, send_out, recv_out,
):
    me = lax.axis_index("heads")
    frame = lax.axis_index("frames")
    plane = me // 4
    nxt = lax.rem(frame + 1, FRAMES)
    prv = lax.rem(frame + FRAMES - 1, FRAMES)
    beside = me + 2 * (1 - 2 * lax.rem(me // 2, 2))

    barrier = pltpu.get_barrier_semaphore()

    lane = lax.rem(me, 4)
    flip = lane + 1 - 2 * lax.rem(lane, 2)
    mates = [flip + 4 * plane, beside, beside + flip - lane]
    for shift in (4, 3, 5, 2, 6, 1, 7):
        there = lax.rem(plane + shift, PLANES) * 4 + lane
        pl.semaphore_signal(barrier, inc=1, device_id=(there, frame), device_id_type=MESH)
    for mate in mates:
        pl.semaphore_signal(barrier, inc=1, device_id=(mate, frame), device_id_type=MESH)
    for other in (prv, nxt):
        pl.semaphore_signal(barrier, inc=1, device_id=(beside, other), device_id_type=MESH)
    fetch = pltpu.make_async_copy(table, nbr, table_sem)
    fetch.start()
    pl.semaphore_wait(barrier, PLANES - 1 + len(mates) + 2)
    for mate in mates:
        pl.semaphore_signal(ready, inc=1, device_id=(mate, frame), device_id_type=MESH)

    mine = pl.ds(pl.multiple_of(me * TOK, TOK), TOK)
    mine_kv = pl.ds(pl.multiple_of(HALO + me * TOK, TOK), TOK)
    first, second = pl.ds(0, HD), pl.ds(HD, HD)
    group = (plane + 2) // 4
    window = ((keys, kk, first), (values, vv, first), (keys_tan, kk, second), (values_tan, vv, second))
    queries = ((query_tan, first), (query, second))

    def column(device):
        return pl.ds(pl.multiple_of(head_of(device, frame) * HD, HD), HD)

    def send_window(which):
        source, buffer, part = window[which]
        target, sem = buffer.at[mine_kv, part], recv_kv.at[which, group]

        def send(step, carry):
            there = partner(me, step)
            pltpu.make_async_remote_copy(
                src_ref=source.at[:, column(there)],
                dst_ref=target,
                send_sem=send_in.at[which],
                recv_sem=sem,
                device_id=(there, frame),
                device_id_type=MESH,
            ).start()
            return carry

        if which == 0:
            lax.fori_loop(HEADS - PLANES, HEADS - 1, send, 0)
            pl.semaphore_wait(ready, len(mates))
            lax.fori_loop(0, HEADS - PLANES, send, 0)
        else:
            lax.fori_loop(0, HEADS - 1, send, 0)
        pltpu.make_async_copy(source.at[:, column(me)], target, sem).start()

    def send_queries(start, stop):
        def send(step, carry):
            there = partner(me, lax.rem(step, 4) * PLANES + step // 4)
            for which, (source, part) in enumerate(queries):
                pltpu.make_async_remote_copy(
                    src_ref=source.at[:, column(there)],
                    dst_ref=qq.at[mine, part],
                    send_sem=send_in.at[4 + which],
                    recv_sem=recv_q.at[plane],
                    device_id=(there, frame),
                    device_id_type=MESH,
                ).start()
            return carry

        lax.fori_loop(start, stop, send, 0)

    copies = []

    def forward(which):
        buffer, part = window[which][1:]
        sides = ((0, HALO, HALO + ROWS, prv), (2, ROWS, 0, nxt))
        for side, (edge, start, landing, other) in enumerate(sides):
            arrived(buffer.at[pl.ds(start, HALO), part], recv_kv.at[which, edge])
            copy = pltpu.make_async_remote_copy(
                src_ref=buffer.at[pl.ds(start, HALO), part],
                dst_ref=buffer.at[pl.ds(landing, HALO), part],
                send_sem=send_halo.at[which, side],
                recv_sem=recv_halo.at[which, side],
                device_id=(beside, other),
                device_id_type=MESH,
            )
            copy.start()
            copies.append(copy)

    send_window(0)
    send_window(1)
    forward(0)
    send_window(2)
    forward(1)
    send_window(3)
    forward(2)
    send_queries(0, 12)
    forward(3)
    send_queries(12, HEADS - 1)
    for which, (source, part) in enumerate(queries):
        pltpu.make_async_copy(source.at[:, column(me)], qq.at[mine, part], recv_q.at[plane]).start()
    for which, (source, buffer, part) in enumerate(window):
        arrived(buffer.at[pl.ds(HALO + 2 * PLANE, 4 * PLANE), part], recv_kv.at[which, 1])
    for copy in copies:
        copy.wait_recv()
    fetch.wait()

    scale = HD**-0.5
    nt = (((1,), (1,)), ((), ()))
    nn = (((1,), (0,)), ((), ()))

    def block_step(step, carry):
        turn = step // 2
        half = (turn + 1) // 2
        shift = jnp.where(lax.rem(turn, 2) == 1, PLANES // 2 - half, PLANES // 2 + half)
        there = lax.rem(plane + shift, PLANES)
        x_lo = lax.rem(lax.rem(me, 4) // 2 + step + 1, 2)
        block = there * 2 + x_lo
        rows = pl.ds(pl.multiple_of(block * BQ, BQ), BQ)

        @pl.when(lax.rem(step, 2) == 0)
        def _():
            arrived(qq.at[pl.ds(pl.multiple_of(there * PLANE, PLANE), PLANE), :], recv_q.at[there])

        both = qq[rows, :]
        q = qq[rows, second]
        wins = []
        for slot in range(WK):
            local = jnp.clip(nbr[slot, block] - frame * BLOCKS + HB, 0, BLOCKS + 2 * HB - 1)
            wins.append(pl.ds(local * BQ, BQ))
        scores = [
            lax.dot_general(q, kk[win, first], nt, preferred_element_type=jnp.float32) for win in wins
        ]
        most = functools.reduce(jnp.maximum, [jnp.max(s, axis=1, keepdims=True) for s in scores])
        total = jnp.zeros((BQ, 1), jnp.float32)
        mean = jnp.zeros((BQ, 1), jnp.float32)
        acc = jnp.zeros((BQ, 2 * HD), jnp.float32)
        acc_w = jnp.zeros((BQ, HD), jnp.float32)
        for s, win in zip(scores, wins):
            p = jnp.exp2((s - most) * (scale * LOG2E))
            st = lax.dot_general(both, kk[win, :], nt, preferred_element_type=jnp.float32)
            w = p * st
            total += jnp.sum(p, axis=1, keepdims=True)
            mean += jnp.sum(w, axis=1, keepdims=True)
            v = vv[win, :]
            acc += lax.dot_general(p.astype(jnp.bfloat16), v, nn, preferred_element_type=jnp.float32)
            acc_w += lax.dot_general(
                w.astype(jnp.bfloat16), v[:, :HD], nn, preferred_element_type=jnp.float32
            )
        inv = 1.0 / total
        o = acc[:, :HD] * inv
        t = (acc[:, HD:] + scale * acc_w) * inv - (scale * mean * inv) * o
        oo[0, rows, :] = o.astype(jnp.bfloat16)
        oo[1, rows, :] = t.astype(jnp.bfloat16)
        home = column(me)
        core = lax.rem(me, 2)
        for flip in (1, 0):
            there_core = lax.rem(core + flip, 2)
            owner = block * 2 + there_core
            piece = pl.ds(pl.multiple_of(owner * TOK, TOK), TOK)
            for which, result in enumerate((out, tan)):

                def remote(which=which, result=result, owner=owner, piece=piece):
                    pltpu.make_async_remote_copy(
                        src_ref=oo.at[which, piece, :],
                        dst_ref=result.at[:, home],
                        send_sem=send_out.at[which],
                        recv_sem=recv_out.at[which],
                        device_id=(owner, frame),
                        device_id_type=MESH,
                    ).start()

                def local(which=which, result=result, piece=piece):
                    pltpu.make_async_copy(
                        oo.at[which, piece, :], result.at[:, home], recv_out.at[which]
                    ).start()

                if flip:
                    remote()
                else:
                    pl.when(step < BLOCKS - 1)(remote)
                    pl.when(step == BLOCKS - 1)(local)
        return carry

    lax.fori_loop(0, BLOCKS, block_step, 0)

    for copy in copies:
        copy.wait_send()
    rest = pl.ds(0, (HEADS - 1) * HD)
    for which in range(6):
        arrived(out.at[:, rest], send_in.at[which])
    for which, result in enumerate((out, tan)):
        arrived(result.at[:, rest], send_out.at[which])
        arrived(result, recv_out.at[which])


def hand_on(out, tan, out_copy, tan_copy, sems):
    copies = [
        pltpu.make_async_copy(out, out_copy, sems.at[0]),
        pltpu.make_async_copy(tan, tan_copy, sems.at[1]),
    ]
    for copy in copies:
        copy.start()
    for copy in copies:
        copy.wait()


def per_device(query, keys, values, query_tan, keys_tan, values_tan, neighbors):
    shape = jax.ShapeDtypeStruct((TOK, HEADS * HD), jnp.bfloat16)
    hbm = pl.BlockSpec(memory_space=pl.ANY)
    dma = pltpu.SemaphoreType.DMA
    results = pl.pallas_call(
        kernel,
        out_shape=(pltpu.VMEM((TOK, HEADS * HD), jnp.bfloat16),) * 2,
        in_specs=[hbm] * 7,
        out_specs=(hbm, hbm),
        scratch_shapes=[
            pltpu.SMEM((WK, BLOCKS), jnp.int32),
            pltpu.VMEM((ROWS + 2 * HALO, 2 * HD), jnp.bfloat16),
            pltpu.VMEM((ROWS + 2 * HALO, 2 * HD), jnp.bfloat16),
            pltpu.VMEM((ROWS, 2 * HD), jnp.bfloat16),
            pltpu.VMEM((2, ROWS, HD), jnp.bfloat16),
            pltpu.SemaphoreType.REGULAR,
            dma,
            dma((6,)),
            dma((4, 3)),
            dma((PLANES,)),
            dma((4, 2)),
            dma((4, 2)),
            dma((2,)),
            dma((2,)),
        ],
        compiler_params=pltpu.CompilerParams(
            collective_id=0, has_side_effects=True, vmem_limit_bytes=56 << 20
        ),
        cost_estimate=pl.CostEstimate(
            flops=7 * 10**9, bytes_accessed=20 << 20, transcendentals=5 * 10**6
        ),
        name="attend",
    )(neighbors.T, query, keys, values, query_tan, keys_tan, values_tan)
    results = [pltpu.with_memory_space_constraint(result, pltpu.VMEM) for result in results]
    return pl.pallas_call(
        hand_on,
        out_shape=(shape, shape),
        in_specs=[pl.BlockSpec(memory_space=pltpu.VMEM)] * 2,
        out_specs=(hbm, hbm),
        scratch_shapes=[dma((2,))],
        name="hand_on",
    )(*results)


def solution(mesh):
    tokens = P(("frames", "heads"), None)
    return jax.shard_map(
        per_device,
        mesh=mesh,
        in_specs=(tokens,) * 6 + (P("frames", None),),
        out_specs=(tokens, tokens),
        check_vma=False,
    )
```

```python
import functools

import jax
import jax.numpy as jnp
from jax import lax
from jax.experimental import pallas as pl
from jax.experimental.pallas import tpu as pltpu
from jax.sharding import PartitionSpec as P

MESH = pl.DeviceIdType.MESH
HD = 128
BQ = 256
WK = 4
HB = 4
HALO = HB * BQ
HEADS = 32
FRAMES = 8
PLANES = 8
TOK = 128
ROWS = HEADS * TOK
PLANE = ROWS // PLANES
BLOCKS = ROWS // BQ
LOG2E = 1.4426950408889634


def partner(me, step):
    turn = lax.rem(step, PLANES)
    half = (turn + 1) // 2
    shift = jnp.where(lax.rem(turn, 2) == 1, PLANES // 2 - half, PLANES // 2 + half)
    plane = lax.rem(me // 4 + shift, PLANES)
    lane = lax.rem(step // PLANES + 1, 4)
    mine = lax.rem(me, 4)
    flip_core = lax.rem(lane, 2)
    flip_x = lane // 2
    core = lax.rem(lax.rem(mine, 2) + flip_core, 2)
    x_lo = lax.rem(mine // 2 + flip_x, 2)
    return plane * 4 + x_lo * 2 + core


def head_of(device, frame):
    x_lo = lax.rem(device // 2, 2)
    return device + 2 * lax.rem(frame, 2) * (1 - 2 * x_lo)


def arrived(ref, sem):
    pltpu.make_async_copy(ref, ref, sem).wait()


def kernel(
    table, query, keys, values, query_tan, keys_tan, values_tan, out, tan,
    nbr, kk, vv, qq, oo, ready, table_sem, send_in, recv_kv, recv_q, send_halo, recv_halo, send_out, recv_out,
):
    me = lax.axis_index("heads")
    frame = lax.axis_index("frames")
    plane = me // 4
    nxt = lax.rem(frame + 1, FRAMES)
    prv = lax.rem(frame + FRAMES - 1, FRAMES)
    beside = me + 2 * (1 - 2 * lax.rem(me // 2, 2))

    barrier = pltpu.get_barrier_semaphore()

    lane = lax.rem(me, 4)
    flip = lane + 1 - 2 * lax.rem(lane, 2)
    mates = [flip + 4 * plane, beside, beside + flip - lane]
    for shift in (4, 3, 5, 2, 6, 1, 7):
        there = lax.rem(plane + shift, PLANES) * 4 + lane
        pl.semaphore_signal(barrier, inc=1, device_id=(there, frame), device_id_type=MESH)
    for mate in mates:
        pl.semaphore_signal(barrier, inc=1, device_id=(mate, frame), device_id_type=MESH)
    for other in (prv, nxt):
        pl.semaphore_signal(barrier, inc=1, device_id=(4 * plane + 3, other), device_id_type=MESH)
    fetch = pltpu.make_async_copy(table, nbr, table_sem)
    fetch.start()
    known = PLANES - 1 + len(mates)
    pl.semaphore_wait(barrier, jnp.where(lane == 3, known + 2 * 4, known))
    for mate in mates:
        pl.semaphore_signal(ready, inc=1, device_id=(mate, frame), device_id_type=MESH)

    mine = pl.ds(pl.multiple_of(me * TOK, TOK), TOK)
    mine_kv = pl.ds(pl.multiple_of(HALO + me * TOK, TOK), TOK)
    first, second = pl.ds(0, HD), pl.ds(HD, HD)
    group = (plane + 2) // 4
    window = ((keys, kk, first), (values, vv, first), (keys_tan, kk, second), (values_tan, vv, second))
    queries = ((query_tan, first), (query, second))

    def column(device):
        return pl.ds(pl.multiple_of(head_of(device, frame) * HD, HD), HD)

    def send_window(which):
        source, buffer, part = window[which]
        target, sem = buffer.at[mine_kv, part], recv_kv.at[which, group]

        def send(step, carry):
            there = partner(me, step)
            pltpu.make_async_remote_copy(
                src_ref=source.at[:, column(there)],
                dst_ref=target,
                send_sem=send_in.at[which],
                recv_sem=sem,
                device_id=(there, frame),
                device_id_type=MESH,
            ).start()
            return carry

        if which == 0:
            lax.fori_loop(HEADS - PLANES, HEADS - 1, send, 0)
            pl.semaphore_wait(ready, len(mates))
            lax.fori_loop(0, HEADS - PLANES, send, 0)
        else:
            lax.fori_loop(0, HEADS - 1, send, 0)
        pltpu.make_async_copy(source.at[:, column(me)], target, sem).start()

    def send_queries(start, stop):
        def send(step, carry):
            there = partner(me, lax.rem(step, 4) * PLANES + step // 4)
            for which, (source, part) in enumerate(queries):
                pltpu.make_async_remote_copy(
                    src_ref=source.at[:, column(there)],
                    dst_ref=qq.at[mine, part],
                    send_sem=send_in.at[4 + which],
                    recv_sem=recv_q.at[plane],
                    device_id=(there, frame),
                    device_id_type=MESH,
                ).start()
            return carry

        lax.fori_loop(start, stop, send, 0)

    copies = []

    def forward(which):
        buffer, part = window[which][1:]
        sides = ((0, HALO, HALO + ROWS, prv), (2, ROWS, 0, nxt))
        for side, (edge, start, landing, other) in enumerate(sides):
            arrived(buffer.at[pl.ds(start, HALO), part], recv_kv.at[which, edge])
            copy = pltpu.make_async_remote_copy(
                src_ref=buffer.at[pl.ds(start, HALO), part],
                dst_ref=buffer.at[pl.ds(landing, HALO), part],
                send_sem=send_halo.at[which, side],
                recv_sem=recv_halo.at[which, side],
                device_id=(beside, other),
                device_id_type=MESH,
            )
            copy.start()
            copies.append(copy)

    send_window(0)
    send_window(1)
    forward(0)
    send_window(2)
    forward(1)
    send_window(3)
    forward(2)
    send_queries(0, 12)
    forward(3)
    send_queries(12, HEADS - 1)
    for which, (source, part) in enumerate(queries):
        pltpu.make_async_copy(source.at[:, column(me)], qq.at[mine, part], recv_q.at[plane]).start()
    for which, (source, buffer, part) in enumerate(window):
        arrived(buffer.at[pl.ds(HALO + 2 * PLANE, 4 * PLANE), part], recv_kv.at[which, 1])
    for copy in copies:
        copy.wait_recv()
    fetch.wait()

    scale = HD**-0.5
    nt = (((1,), (1,)), ((), ()))
    nn = (((1,), (0,)), ((), ()))

    def block_step(step, carry):
        turn = step // 2
        half = (turn + 1) // 2
        shift = jnp.where(lax.rem(turn, 2) == 1, PLANES // 2 - half, PLANES // 2 + half)
        there = lax.rem(plane + shift, PLANES)
        x_lo = lax.rem(lax.rem(me, 4) // 2 + step + 1, 2)
        block = there * 2 + x_lo
        rows = pl.ds(pl.multiple_of(block * BQ, BQ), BQ)

        @pl.when(lax.rem(step, 2) == 0)
        def _():
            arrived(qq.at[pl.ds(pl.multiple_of(there * PLANE, PLANE), PLANE), :], recv_q.at[there])

        both = qq[rows, :]
        q = qq[rows, second]
        wins = []
        for slot in range(WK):
            local = jnp.clip(nbr[slot, block] - frame * BLOCKS + HB, 0, BLOCKS + 2 * HB - 1)
            wins.append(pl.ds(local * BQ, BQ))
        scores = [
            lax.dot_general(q, kk[win, first], nt, preferred_element_type=jnp.float32) for win in wins
        ]
        most = functools.reduce(jnp.maximum, [jnp.max(s, axis=1, keepdims=True) for s in scores])
        total = jnp.zeros((BQ, 1), jnp.float32)
        mean = jnp.zeros((BQ, 1), jnp.float32)
        acc = jnp.zeros((BQ, 2 * HD), jnp.float32)
        acc_w = jnp.zeros((BQ, HD), jnp.float32)
        for s, win in zip(scores, wins):
            p = jnp.exp2((s - most) * (scale * LOG2E))
            st = lax.dot_general(both, kk[win, :], nt, preferred_element_type=jnp.float32)
            w = p * st
            total += jnp.sum(p, axis=1, keepdims=True)
            mean += jnp.sum(w, axis=1, keepdims=True)
            v = vv[win, :]
            acc += lax.dot_general(p.astype(jnp.bfloat16), v, nn, preferred_element_type=jnp.float32)
            acc_w += lax.dot_general(
                w.astype(jnp.bfloat16), v[:, :HD], nn, preferred_element_type=jnp.float32
            )
        inv = 1.0 / total
        o = acc[:, :HD] * inv
        t = (acc[:, HD:] + scale * acc_w) * inv - (scale * mean * inv) * o
        oo[0, rows, :] = o.astype(jnp.bfloat16)
        oo[1, rows, :] = t.astype(jnp.bfloat16)
        home = column(me)
        core = lax.rem(me, 2)
        for flip in (1, 0):
            there_core = lax.rem(core + flip, 2)
            owner = block * 2 + there_core
            piece = pl.ds(pl.multiple_of(owner * TOK, TOK), TOK)
            for which, result in enumerate((out, tan)):

                def remote(which=which, result=result, owner=owner, piece=piece):
                    pltpu.make_async_remote_copy(
                        src_ref=oo.at[which, piece, :],
                        dst_ref=result.at[:, home],
                        send_sem=send_out.at[which],
                        recv_sem=recv_out.at[which],
                        device_id=(owner, frame),
                        device_id_type=MESH,
                    ).start()

                def local(which=which, result=result, piece=piece):
                    pltpu.make_async_copy(
                        oo.at[which, piece, :], result.at[:, home], recv_out.at[which]
                    ).start()

                if flip:
                    remote()
                else:
                    pl.when(step < BLOCKS - 1)(remote)
                    pl.when(step == BLOCKS - 1)(local)
        return carry

    lax.fori_loop(0, BLOCKS, block_step, 0)

    for copy in copies:
        copy.wait_send()
    rest = pl.ds(0, (HEADS - 1) * HD)
    for which in range(6):
        arrived(out.at[:, rest], send_in.at[which])
    for which, result in enumerate((out, tan)):
        arrived(result.at[:, rest], send_out.at[which])
        arrived(result, recv_out.at[which])


def hand_on(out, tan, out_copy, tan_copy, sems):
    copies = [
        pltpu.make_async_copy(out, out_copy, sems.at[0]),
        pltpu.make_async_copy(tan, tan_copy, sems.at[1]),
    ]
    for copy in copies:
        copy.start()
    for copy in copies:
        copy.wait()


def per_device(query, keys, values, query_tan, keys_tan, values_tan, neighbors):
    shape = jax.ShapeDtypeStruct((TOK, HEADS * HD), jnp.bfloat16)
    hbm = pl.BlockSpec(memory_space=pl.ANY)
    dma = pltpu.SemaphoreType.DMA
    results = pl.pallas_call(
        kernel,
        out_shape=(pltpu.VMEM((TOK, HEADS * HD), jnp.bfloat16),) * 2,
        in_specs=[hbm] * 7,
        out_specs=(hbm, hbm),
        scratch_shapes=[
            pltpu.SMEM((WK, BLOCKS), jnp.int32),
            pltpu.VMEM((ROWS + 2 * HALO, 2 * HD), jnp.bfloat16),
            pltpu.VMEM((ROWS + 2 * HALO, 2 * HD), jnp.bfloat16),
            pltpu.VMEM((ROWS, 2 * HD), jnp.bfloat16),
            pltpu.VMEM((2, ROWS, HD), jnp.bfloat16),
            pltpu.SemaphoreType.REGULAR,
            dma,
            dma((6,)),
            dma((4, 3)),
            dma((PLANES,)),
            dma((4, 2)),
            dma((4, 2)),
            dma((2,)),
            dma((2,)),
        ],
        compiler_params=pltpu.CompilerParams(
            collective_id=0, has_side_effects=True, vmem_limit_bytes=56 << 20
        ),
        cost_estimate=pl.CostEstimate(
            flops=7 * 10**9, bytes_accessed=20 << 20, transcendentals=5 * 10**6
        ),
        name="attend",
    )(neighbors.T, query, keys, values, query_tan, keys_tan, values_tan)
    results = [pltpu.with_memory_space_constraint(result, pltpu.VMEM) for result in results]
    return pl.pallas_call(
        hand_on,
        out_shape=(shape, shape),
        in_specs=[pl.BlockSpec(memory_space=pltpu.VMEM)] * 2,
        out_specs=(hbm, hbm),
        scratch_shapes=[dma((2,))],
        name="hand_on",
    )(*results)


def solution(mesh):
    tokens = P(("frames", "heads"), None)
    return jax.shard_map(
        per_device,
        mesh=mesh,
        in_specs=(tokens,) * 6 + (P("frames", None),),
        out_specs=(tokens, tokens),
        check_vma=False,
    )
```

```python
import functools

import jax
import jax.numpy as jnp
from jax import lax
from jax.experimental import pallas as pl
from jax.experimental.pallas import tpu as pltpu
from jax.sharding import PartitionSpec as P

MESH = pl.DeviceIdType.MESH
HD = 128
BQ = 256
WK = 4
HB = 4
HALO = HB * BQ
HEADS = 32
FRAMES = 8
PLANES = 8
TOK = 128
ROWS = HEADS * TOK
PLANE = ROWS // PLANES
BLOCKS = ROWS // BQ
LOG2E = 1.4426950408889634


def partner(me, step):
    turn = lax.rem(step, PLANES)
    half = (turn + 1) // 2
    shift = jnp.where(lax.rem(turn, 2) == 1, PLANES // 2 - half, PLANES // 2 + half)
    plane = lax.rem(me // 4 + shift, PLANES)
    lane = lax.rem(step // PLANES + 1, 4)
    mine = lax.rem(me, 4)
    flip_core = lax.rem(lane, 2)
    flip_x = lane // 2
    core = lax.rem(lax.rem(mine, 2) + flip_core, 2)
    x_lo = lax.rem(mine // 2 + flip_x, 2)
    return plane * 4 + x_lo * 2 + core


def head_of(device, frame):
    x_lo = lax.rem(device // 2, 2)
    return device + 2 * lax.rem(frame, 2) * (1 - 2 * x_lo)


def arrived(ref, sem):
    pltpu.make_async_copy(ref, ref, sem).wait()


def kernel(
    table, query, keys, values, query_tan, keys_tan, values_tan, out, tan,
    nbr, kk, vv, qq, oo, ready, table_sem, send_in, recv_kv, recv_q, send_halo, recv_halo, send_out, recv_out,
):
    me = lax.axis_index("heads")
    frame = lax.axis_index("frames")
    plane = me // 4
    nxt = lax.rem(frame + 1, FRAMES)
    prv = lax.rem(frame + FRAMES - 1, FRAMES)
    beside = me + 2 * (1 - 2 * lax.rem(me // 2, 2))

    barrier = pltpu.get_barrier_semaphore()

    lane = lax.rem(me, 4)
    flip = lane + 1 - 2 * lax.rem(lane, 2)
    mates = [flip + 4 * plane, beside, beside + flip - lane]
    for shift in (4, 3, 5, 2, 6, 1, 7):
        there = lax.rem(plane + shift, PLANES) * 4 + lane
        pl.semaphore_signal(barrier, inc=1, device_id=(there, frame), device_id_type=MESH)
    for mate in mates:
        pl.semaphore_signal(barrier, inc=1, device_id=(mate, frame), device_id_type=MESH)
    for other in (prv, nxt):
        pl.semaphore_signal(barrier, inc=1, device_id=(4 * plane + 3, other), device_id_type=MESH)
    fetch = pltpu.make_async_copy(table, nbr, table_sem)
    fetch.start()
    known = PLANES - 1 + len(mates)
    pl.semaphore_wait(barrier, jnp.where(lane == 3, known + 2 * 4, known))
    for mate in mates:
        pl.semaphore_signal(ready, inc=1, device_id=(mate, frame), device_id_type=MESH)

    mine = pl.ds(pl.multiple_of(me * TOK, TOK), TOK)
    mine_kv = pl.ds(pl.multiple_of(HALO + me * TOK, TOK), TOK)
    first, second = pl.ds(0, HD), pl.ds(HD, HD)
    group = (plane + 2) // 4
    window = ((keys, kk, first), (values, vv, first), (keys_tan, kk, second), (values_tan, vv, second))
    queries = ((query_tan, first), (query, second))

    def column(device):
        return pl.ds(pl.multiple_of(head_of(device, frame) * HD, HD), HD)

    def send_window(which):
        source, buffer, part = window[which]
        target, sem = buffer.at[mine_kv, part], recv_kv.at[which, group]

        def send(step, carry):
            there = partner(me, step)
            pltpu.make_async_remote_copy(
                src_ref=source.at[:, column(there)],
                dst_ref=target,
                send_sem=send_in.at[which],
                recv_sem=sem,
                device_id=(there, frame),
                device_id_type=MESH,
            ).start()
            return carry

        if which == 0:
            lax.fori_loop(HEADS - PLANES, HEADS - 1, send, 0)
            pl.semaphore_wait(ready, len(mates))
            lax.fori_loop(0, HEADS - PLANES, send, 0)
        else:
            lax.fori_loop(0, HEADS - 1, send, 0)
        pltpu.make_async_copy(source.at[:, column(me)], target, sem).start()

    def send_queries(start, stop):
        def send(step, carry):
            there = partner(me, lax.rem(step, 4) * PLANES + step // 4)
            for which, (source, part) in enumerate(queries):
                pltpu.make_async_remote_copy(
                    src_ref=source.at[:, column(there)],
                    dst_ref=qq.at[mine, part],
                    send_sem=send_in.at[4 + which],
                    recv_sem=recv_q.at[plane],
                    device_id=(there, frame),
                    device_id_type=MESH,
                ).start()
            return carry

        lax.fori_loop(start, stop, send, 0)

    copies = []

    def forward(which):
        buffer, part = window[which][1:]
        sides = ((0, HALO, HALO + ROWS, prv), (2, ROWS, 0, nxt))
        for side, (edge, start, landing, other) in enumerate(sides):
            arrived(buffer.at[pl.ds(start, HALO), part], recv_kv.at[which, edge])
            copy = pltpu.make_async_remote_copy(
                src_ref=buffer.at[pl.ds(start, HALO), part],
                dst_ref=buffer.at[pl.ds(landing, HALO), part],
                send_sem=send_halo.at[which, side],
                recv_sem=recv_halo.at[which, side],
                device_id=(beside, other),
                device_id_type=MESH,
            )
            copy.start()
            copies.append(copy)

    send_window(0)
    send_window(1)
    forward(0)
    send_window(2)
    forward(1)
    send_window(3)
    forward(2)
    send_queries(0, 12)
    forward(3)
    send_queries(12, HEADS - 1)
    for which, (source, part) in enumerate(queries):
        pltpu.make_async_copy(source.at[:, column(me)], qq.at[mine, part], recv_q.at[plane]).start()
    for which, (source, buffer, part) in enumerate(window):
        arrived(buffer.at[pl.ds(HALO + 2 * PLANE, 4 * PLANE), part], recv_kv.at[which, 1])
    for copy in copies:
        copy.wait_recv()
    fetch.wait()

    scale = HD**-0.5
    nt = (((1,), (1,)), ((), ()))
    nn = (((1,), (0,)), ((), ()))

    def block_step(step, carry):
        turn = step // 2
        half = (turn + 1) // 2
        shift = jnp.where(lax.rem(turn, 2) == 1, PLANES // 2 - half, PLANES // 2 + half)
        there = lax.rem(plane + shift, PLANES)
        x_lo = lax.rem(lax.rem(me, 4) // 2 + step + 1, 2)
        block = there * 2 + x_lo
        rows = pl.ds(pl.multiple_of(block * BQ, BQ), BQ)

        @pl.when(lax.rem(step, 2) == 0)
        def _():
            arrived(qq.at[pl.ds(pl.multiple_of(there * PLANE, PLANE), PLANE), :], recv_q.at[there])

        both = qq[rows, :]
        q = qq[rows, second]
        wins = []
        for slot in range(WK):
            local = jnp.clip(nbr[slot, block] - frame * BLOCKS + HB, 0, BLOCKS + 2 * HB - 1)
            wins.append(pl.ds(local * BQ, BQ))
        scores = [
            lax.dot_general(q, kk[win, first], nt, preferred_element_type=jnp.float32) for win in wins
        ]
        most = functools.reduce(jnp.maximum, [jnp.max(s, axis=1, keepdims=True) for s in scores])
        weights = [jnp.exp2((s - most) * (scale * LOG2E)) for s in scores]
        inv = 1.0 / functools.reduce(jnp.add, [jnp.sum(p, axis=1, keepdims=True) for p in weights])
        mean = jnp.zeros((BQ, 1), jnp.float32)
        acc = jnp.zeros((BQ, 2 * HD), jnp.float32)
        acc_w = jnp.zeros((BQ, HD), jnp.float32)
        for p, win in zip(weights, wins):
            p = p * inv
            st = lax.dot_general(both, kk[win, :], nt, preferred_element_type=jnp.float32)
            w = p * (st * scale)
            mean += jnp.sum(w, axis=1, keepdims=True)
            v = vv[win, :]
            acc += lax.dot_general(p.astype(jnp.bfloat16), v, nn, preferred_element_type=jnp.float32)
            acc_w += lax.dot_general(
                w.astype(jnp.bfloat16), v[:, :HD], nn, preferred_element_type=jnp.float32
            )
        o = acc[:, :HD]
        t = acc[:, HD:] + acc_w - mean * o
        oo[0, rows, :] = o.astype(jnp.bfloat16)
        oo[1, rows, :] = t.astype(jnp.bfloat16)
        home = column(me)
        core = lax.rem(me, 2)
        for flip in (1, 0):
            there_core = lax.rem(core + flip, 2)
            owner = block * 2 + there_core
            piece = pl.ds(pl.multiple_of(owner * TOK, TOK), TOK)
            for which, result in enumerate((out, tan)):

                def remote(which=which, result=result, owner=owner, piece=piece):
                    pltpu.make_async_remote_copy(
                        src_ref=oo.at[which, piece, :],
                        dst_ref=result.at[:, home],
                        send_sem=send_out.at[which],
                        recv_sem=recv_out.at[which],
                        device_id=(owner, frame),
                        device_id_type=MESH,
                    ).start()

                def local(which=which, result=result, piece=piece):
                    pltpu.make_async_copy(
                        oo.at[which, piece, :], result.at[:, home], recv_out.at[which]
                    ).start()

                if flip:
                    remote()
                else:
                    pl.when(step < BLOCKS - 1)(remote)
                    pl.when(step == BLOCKS - 1)(local)
        return carry

    lax.fori_loop(0, BLOCKS, block_step, 0)

    for copy in copies:
        copy.wait_send()
    rest = pl.ds(0, (HEADS - 1) * HD)
    for which in range(6):
        arrived(out.at[:, rest], send_in.at[which])
    for which, result in enumerate((out, tan)):
        arrived(result.at[:, rest], send_out.at[which])
        arrived(result, recv_out.at[which])


def hand_on(out, tan, out_copy, tan_copy, sems):
    copies = [
        pltpu.make_async_copy(out, out_copy, sems.at[0]),
        pltpu.make_async_copy(tan, tan_copy, sems.at[1]),
    ]
    for copy in copies:
        copy.start()
    for copy in copies:
        copy.wait()


def per_device(query, keys, values, query_tan, keys_tan, values_tan, neighbors):
    shape = jax.ShapeDtypeStruct((TOK, HEADS * HD), jnp.bfloat16)
    hbm = pl.BlockSpec(memory_space=pl.ANY)
    dma = pltpu.SemaphoreType.DMA
    results = pl.pallas_call(
        kernel,
        out_shape=(pltpu.VMEM((TOK, HEADS * HD), jnp.bfloat16),) * 2,
        in_specs=[hbm] * 7,
        out_specs=(hbm, hbm),
        scratch_shapes=[
            pltpu.SMEM((WK, BLOCKS), jnp.int32),
            pltpu.VMEM((ROWS + 2 * HALO, 2 * HD), jnp.bfloat16),
            pltpu.VMEM((ROWS + 2 * HALO, 2 * HD), jnp.bfloat16),
            pltpu.VMEM((ROWS, 2 * HD), jnp.bfloat16),
            pltpu.VMEM((2, ROWS, HD), jnp.bfloat16),
            pltpu.SemaphoreType.REGULAR,
            dma,
            dma((6,)),
            dma((4, 3)),
            dma((PLANES,)),
            dma((4, 2)),
            dma((4, 2)),
            dma((2,)),
            dma((2,)),
        ],
        compiler_params=pltpu.CompilerParams(
            collective_id=0, has_side_effects=True, vmem_limit_bytes=56 << 20
        ),
        cost_estimate=pl.CostEstimate(
            flops=7 * 10**9, bytes_accessed=20 << 20, transcendentals=5 * 10**6
        ),
        name="attend",
    )(neighbors.T, query, keys, values, query_tan, keys_tan, values_tan)
    results = [pltpu.with_memory_space_constraint(result, pltpu.VMEM) for result in results]
    return pl.pallas_call(
        hand_on,
        out_shape=(shape, shape),
        in_specs=[pl.BlockSpec(memory_space=pltpu.VMEM)] * 2,
        out_specs=(hbm, hbm),
        scratch_shapes=[dma((2,))],
        name="hand_on",
    )(*results)


def solution(mesh):
    tokens = P(("frames", "heads"), None)
    return jax.shard_map(
        per_device,
        mesh=mesh,
        in_specs=(tokens,) * 6 + (P("frames", None),),
        out_specs=(tokens, tokens),
        check_vma=False,
    )
```

```python
import functools

import jax
import jax.numpy as jnp
from jax import lax
from jax.experimental import pallas as pl
from jax.experimental.pallas import tpu as pltpu
from jax.sharding import PartitionSpec as P

MESH = pl.DeviceIdType.MESH
HD = 128
BQ = 256
WK = 4
HB = 4
HALO = HB * BQ
HEADS = 32
FRAMES = 8
PLANES = 8
TOK = 128
ROWS = HEADS * TOK
PLANE = ROWS // PLANES
BLOCKS = ROWS // BQ
LOG2E = 1.4426950408889634


def partner(me, step):
    turn = lax.rem(step, PLANES)
    half = (turn + 1) // 2
    shift = jnp.where(lax.rem(turn, 2) == 1, PLANES // 2 - half, PLANES // 2 + half)
    plane = lax.rem(me // 4 + shift, PLANES)
    lane = lax.rem(step // PLANES + 1, 4)
    mine = lax.rem(me, 4)
    flip_core = lax.rem(lane, 2)
    flip_x = lane // 2
    core = lax.rem(lax.rem(mine, 2) + flip_core, 2)
    x_lo = lax.rem(mine // 2 + flip_x, 2)
    return plane * 4 + x_lo * 2 + core


def head_of(device, frame):
    x_lo = lax.rem(device // 2, 2)
    return device + 2 * lax.rem(frame, 2) * (1 - 2 * x_lo)


def arrived(ref, sem):
    pltpu.make_async_copy(ref, ref, sem).wait()


def kernel(
    table, query, keys, values, query_tan, keys_tan, values_tan, out, tan,
    nbr, kk, vv, qq, oo, ready, table_sem, send_in, recv_kv, recv_q, send_halo, recv_halo, send_out, recv_out,
):
    me = lax.axis_index("heads")
    frame = lax.axis_index("frames")
    plane = me // 4
    nxt = lax.rem(frame + 1, FRAMES)
    prv = lax.rem(frame + FRAMES - 1, FRAMES)
    beside = me + 2 * (1 - 2 * lax.rem(me // 2, 2))

    barrier = pltpu.get_barrier_semaphore()

    lane = lax.rem(me, 4)
    flip = lane + 1 - 2 * lax.rem(lane, 2)
    mates = [flip + 4 * plane, beside, beside + flip - lane]
    for shift in (4, 3, 5, 2, 6, 1, 7):
        there = lax.rem(plane + shift, PLANES) * 4 + lane
        pl.semaphore_signal(barrier, inc=1, device_id=(there, frame), device_id_type=MESH)
    for mate in mates:
        pl.semaphore_signal(barrier, inc=1, device_id=(mate, frame), device_id_type=MESH)
    for other in (prv, nxt):
        pl.semaphore_signal(barrier, inc=1, device_id=(4 * plane + 3, other), device_id_type=MESH)
    fetch = pltpu.make_async_copy(table, nbr, table_sem)
    fetch.start()
    known = PLANES - 1 + len(mates)
    pl.semaphore_wait(barrier, jnp.where(lane == 3, known + 2 * 4, known))
    for mate in mates:
        pl.semaphore_signal(ready, inc=1, device_id=(mate, frame), device_id_type=MESH)

    mine = pl.ds(pl.multiple_of(me * TOK, TOK), TOK)
    mine_kv = pl.ds(pl.multiple_of(HALO + me * TOK, TOK), TOK)
    first, second = pl.ds(0, HD), pl.ds(HD, HD)
    group = (plane + 2) // 4
    window = ((keys, kk, first), (values, vv, first), (keys_tan, kk, second), (values_tan, vv, second))
    queries = ((query_tan, first), (query, second))

    def column(device):
        return pl.ds(pl.multiple_of(head_of(device, frame) * HD, HD), HD)

    def send_window(which):
        source, buffer, part = window[which]
        target, sem = buffer.at[mine_kv, part], recv_kv.at[which, group]

        def send(step, carry):
            there = partner(me, step)
            pltpu.make_async_remote_copy(
                src_ref=source.at[:, column(there)],
                dst_ref=target,
                send_sem=send_in.at[which],
                recv_sem=sem,
                device_id=(there, frame),
                device_id_type=MESH,
            ).start()
            return carry

        if which == 0:
            lax.fori_loop(HEADS - PLANES, HEADS - 1, send, 0)
            pl.semaphore_wait(ready, len(mates))
            lax.fori_loop(0, HEADS - PLANES, send, 0)
        else:
            lax.fori_loop(0, HEADS - 1, send, 0)
        pltpu.make_async_copy(source.at[:, column(me)], target, sem).start()

    def send_queries(which):
        source, part = queries[which]

        def send(step, carry):
            there = partner(me, lax.rem(step, 4) * PLANES + step // 4)
            pltpu.make_async_remote_copy(
                src_ref=source.at[:, column(there)],
                dst_ref=qq.at[mine, part],
                send_sem=send_in.at[4 + which],
                recv_sem=recv_q.at[plane],
                device_id=(there, frame),
                device_id_type=MESH,
            ).start()
            return carry

        lax.fori_loop(0, HEADS - 1, send, 0)

    copies = []

    def forward(which):
        buffer, part = window[which][1:]
        sides = ((0, HALO, HALO + ROWS, prv), (2, ROWS, 0, nxt))
        for side, (edge, start, landing, other) in enumerate(sides):
            arrived(buffer.at[pl.ds(start, HALO), part], recv_kv.at[which, edge])
            copy = pltpu.make_async_remote_copy(
                src_ref=buffer.at[pl.ds(start, HALO), part],
                dst_ref=buffer.at[pl.ds(landing, HALO), part],
                send_sem=send_halo.at[which, side],
                recv_sem=recv_halo.at[which, side],
                device_id=(beside, other),
                device_id_type=MESH,
            )
            copy.start()
            copies.append(copy)

    send_window(0)
    send_window(1)
    forward(0)
    send_window(2)
    forward(1)
    send_window(3)
    forward(2)
    send_queries(0)
    forward(3)
    send_queries(1)
    for which, (source, part) in enumerate(queries):
        pltpu.make_async_copy(source.at[:, column(me)], qq.at[mine, part], recv_q.at[plane]).start()
    for which, (source, buffer, part) in enumerate(window):
        arrived(buffer.at[pl.ds(HALO + 2 * PLANE, 4 * PLANE), part], recv_kv.at[which, 1])
    for copy in copies:
        copy.wait_recv()
    fetch.wait()

    scale = HD**-0.5
    nt = (((1,), (1,)), ((), ()))
    nn = (((1,), (0,)), ((), ()))

    def block_step(step, carry):
        turn = step // 2
        half = (turn + 1) // 2
        shift = jnp.where(lax.rem(turn, 2) == 1, PLANES // 2 - half, PLANES // 2 + half)
        there = lax.rem(plane + shift, PLANES)
        x_lo = lax.rem(lax.rem(me, 4) // 2 + step + 1, 2)
        block = there * 2 + x_lo
        rows = pl.ds(pl.multiple_of(block * BQ, BQ), BQ)

        @pl.when(lax.rem(step, 2) == 0)
        def _():
            arrived(qq.at[pl.ds(pl.multiple_of(there * PLANE, PLANE), PLANE), :], recv_q.at[there])

        both = qq[rows, :]
        q = qq[rows, second]
        wins = []
        for slot in range(WK):
            local = jnp.clip(nbr[slot, block] - frame * BLOCKS + HB, 0, BLOCKS + 2 * HB - 1)
            wins.append(pl.ds(local * BQ, BQ))
        scores = [
            lax.dot_general(q, kk[win, first], nt, preferred_element_type=jnp.float32) for win in wins
        ]
        most = functools.reduce(jnp.maximum, [jnp.max(s, axis=1, keepdims=True) for s in scores])
        weights = [jnp.exp2((s - most) * (scale * LOG2E)) for s in scores]
        inv = 1.0 / functools.reduce(jnp.add, [jnp.sum(p, axis=1, keepdims=True) for p in weights])
        mean = jnp.zeros((BQ, 1), jnp.float32)
        acc = jnp.zeros((BQ, 2 * HD), jnp.float32)
        acc_w = jnp.zeros((BQ, HD), jnp.float32)
        for p, win in zip(weights, wins):
            p = p * inv
            st = lax.dot_general(both, kk[win, :], nt, preferred_element_type=jnp.float32)
            w = p * (st * scale)
            mean += jnp.sum(w, axis=1, keepdims=True)
            v = vv[win, :]
            acc += lax.dot_general(p.astype(jnp.bfloat16), v, nn, preferred_element_type=jnp.float32)
            acc_w += lax.dot_general(
                w.astype(jnp.bfloat16), v[:, :HD], nn, preferred_element_type=jnp.float32
            )
        o = acc[:, :HD]
        t = acc[:, HD:] + acc_w - mean * o
        oo[0, rows, :] = o.astype(jnp.bfloat16)
        oo[1, rows, :] = t.astype(jnp.bfloat16)
        home = column(me)
        core = lax.rem(me, 2)
        for flip in (1, 0):
            there_core = lax.rem(core + flip, 2)
            owner = block * 2 + there_core
            piece = pl.ds(pl.multiple_of(owner * TOK, TOK), TOK)
            for which, result in enumerate((out, tan)):

                def remote(which=which, result=result, owner=owner, piece=piece):
                    pltpu.make_async_remote_copy(
                        src_ref=oo.at[which, piece, :],
                        dst_ref=result.at[:, home],
                        send_sem=send_out.at[which],
                        recv_sem=recv_out.at[which],
                        device_id=(owner, frame),
                        device_id_type=MESH,
                    ).start()

                def local(which=which, result=result, piece=piece):
                    pltpu.make_async_copy(
                        oo.at[which, piece, :], result.at[:, home], recv_out.at[which]
                    ).start()

                if flip:
                    remote()
                else:
                    pl.when(step < BLOCKS - 1)(remote)
                    pl.when(step == BLOCKS - 1)(local)
        return carry

    lax.fori_loop(0, BLOCKS, block_step, 0)

    for copy in copies:
        copy.wait_send()
    rest = pl.ds(0, (HEADS - 1) * HD)
    for which in range(6):
        arrived(out.at[:, rest], send_in.at[which])
    for which, result in enumerate((out, tan)):
        arrived(result.at[:, rest], send_out.at[which])
        arrived(result, recv_out.at[which])


def hand_on(out, tan, out_copy, tan_copy, sems):
    copies = [
        pltpu.make_async_copy(out, out_copy, sems.at[0]),
        pltpu.make_async_copy(tan, tan_copy, sems.at[1]),
    ]
    for copy in copies:
        copy.start()
    for copy in copies:
        copy.wait()


def per_device(query, keys, values, query_tan, keys_tan, values_tan, neighbors):
    shape = jax.ShapeDtypeStruct((TOK, HEADS * HD), jnp.bfloat16)
    hbm = pl.BlockSpec(memory_space=pl.ANY)
    dma = pltpu.SemaphoreType.DMA
    results = pl.pallas_call(
        kernel,
        out_shape=(pltpu.VMEM((TOK, HEADS * HD), jnp.bfloat16),) * 2,
        in_specs=[hbm] * 7,
        out_specs=(hbm, hbm),
        scratch_shapes=[
            pltpu.SMEM((WK, BLOCKS), jnp.int32),
            pltpu.VMEM((ROWS + 2 * HALO, 2 * HD), jnp.bfloat16),
            pltpu.VMEM((ROWS + 2 * HALO, 2 * HD), jnp.bfloat16),
            pltpu.VMEM((ROWS, 2 * HD), jnp.bfloat16),
            pltpu.VMEM((2, ROWS, HD), jnp.bfloat16),
            pltpu.SemaphoreType.REGULAR,
            dma,
            dma((6,)),
            dma((4, 3)),
            dma((PLANES,)),
            dma((4, 2)),
            dma((4, 2)),
            dma((2,)),
            dma((2,)),
        ],
        compiler_params=pltpu.CompilerParams(
            collective_id=0, has_side_effects=True, vmem_limit_bytes=56 << 20
        ),
        cost_estimate=pl.CostEstimate(
            flops=7 * 10**9, bytes_accessed=20 << 20, transcendentals=5 * 10**6
        ),
        name="attend",
    )(neighbors.T, query, keys, values, query_tan, keys_tan, values_tan)
    results = [pltpu.with_memory_space_constraint(result, pltpu.VMEM) for result in results]
    return pl.pallas_call(
        hand_on,
        out_shape=(shape, shape),
        in_specs=[pl.BlockSpec(memory_space=pltpu.VMEM)] * 2,
        out_specs=(hbm, hbm),
        scratch_shapes=[dma((2,))],
        name="hand_on",
    )(*results)


def solution(mesh):
    tokens = P(("frames", "heads"), None)
    return jax.shard_map(
        per_device,
        mesh=mesh,
        in_specs=(tokens,) * 6 + (P("frames", None),),
        out_specs=(tokens, tokens),
        check_vma=False,
    )
```

```python
import functools

import jax
import jax.numpy as jnp
from jax import lax
from jax.experimental import pallas as pl
from jax.experimental.pallas import tpu as pltpu
from jax.sharding import PartitionSpec as P

MESH = pl.DeviceIdType.MESH
HD = 128
BQ = 256
WK = 4
HB = 4
HALO = HB * BQ
HEADS = 32
FRAMES = 8
PLANES = 8
TOK = 128
ROWS = HEADS * TOK
PLANE = ROWS // PLANES
BLOCKS = ROWS // BQ
LOG2E = 1.4426950408889634


def partner(me, step):
    turn = lax.rem(step, PLANES)
    half = (turn + 1) // 2
    shift = jnp.where(lax.rem(turn, 2) == 1, PLANES // 2 - half, PLANES // 2 + half)
    plane = lax.rem(me // 4 + shift, PLANES)
    lane = lax.rem(step // PLANES + 1, 4)
    mine = lax.rem(me, 4)
    flip_core = lax.rem(lane, 2)
    flip_x = lane // 2
    core = lax.rem(lax.rem(mine, 2) + flip_core, 2)
    x_lo = lax.rem(mine // 2 + flip_x, 2)
    return plane * 4 + x_lo * 2 + core


def head_of(device, frame):
    x_lo = lax.rem(device // 2, 2)
    return device + 2 * lax.rem(frame, 2) * (1 - 2 * x_lo)


def arrived(ref, sem):
    pltpu.make_async_copy(ref, ref, sem).wait()


def kernel(
    table, query, keys, values, query_tan, keys_tan, values_tan, out, tan,
    nbr, kk, vv, qq, oo, ready, table_sem, send_in, recv_kv, recv_q, send_halo, recv_halo, send_out, recv_out,
):
    me = lax.axis_index("heads")
    frame = lax.axis_index("frames")
    plane = me // 4
    nxt = lax.rem(frame + 1, FRAMES)
    prv = lax.rem(frame + FRAMES - 1, FRAMES)
    beside = me + 2 * (1 - 2 * lax.rem(me // 2, 2))

    barrier = pltpu.get_barrier_semaphore()

    lane = lax.rem(me, 4)
    flip = lane + 1 - 2 * lax.rem(lane, 2)
    mates = [flip + 4 * plane, beside, beside + flip - lane]
    for shift in (4, 3, 5, 2, 6, 1, 7):
        there = lax.rem(plane + shift, PLANES) * 4 + lane
        pl.semaphore_signal(barrier, inc=1, device_id=(there, frame), device_id_type=MESH)
    for mate in mates:
        pl.semaphore_signal(barrier, inc=1, device_id=(mate, frame), device_id_type=MESH)
    for other in (prv, nxt):
        pl.semaphore_signal(barrier, inc=1, device_id=(4 * plane + 3, other), device_id_type=MESH)
    fetch = pltpu.make_async_copy(table, nbr, table_sem)
    fetch.start()
    known = PLANES - 1 + len(mates)
    pl.semaphore_wait(barrier, jnp.where(lane == 3, known + 2 * 4, known))
    for mate in mates:
        pl.semaphore_signal(ready, inc=1, device_id=(mate, frame), device_id_type=MESH)

    mine = pl.ds(pl.multiple_of(me * TOK, TOK), TOK)
    mine_kv = pl.ds(pl.multiple_of(HALO + me * TOK, TOK), TOK)
    first, second = pl.ds(0, HD), pl.ds(HD, HD)
    group = (plane + 2) // 4
    window = ((keys, kk, first), (values, vv, first), (keys_tan, kk, second), (values_tan, vv, second))
    queries = ((query_tan, first), (query, second))

    def column(device):
        return pl.ds(pl.multiple_of(head_of(device, frame) * HD, HD), HD)

    def send_window(which):
        source, buffer, part = window[which]
        target, sem = buffer.at[mine_kv, part], recv_kv.at[which, group]

        def send(step, carry):
            there = partner(me, step)
            pltpu.make_async_remote_copy(
                src_ref=source.at[:, column(there)],
                dst_ref=target,
                send_sem=send_in.at[which],
                recv_sem=sem,
                device_id=(there, frame),
                device_id_type=MESH,
            ).start()
            return carry

        if which == 0:
            lax.fori_loop(HEADS - PLANES, HEADS - 1, send, 0)
            pl.semaphore_wait(ready, len(mates))
            lax.fori_loop(0, HEADS - PLANES, send, 0)
        else:
            lax.fori_loop(0, HEADS - 1, send, 0)
        pltpu.make_async_copy(source.at[:, column(me)], target, sem).start()

    def send_queries(which):
        source, part = queries[which]

        def send(step, carry):
            there = partner(me, lax.rem(step, 4) * PLANES + step // 4)
            pltpu.make_async_remote_copy(
                src_ref=source.at[:, column(there)],
                dst_ref=qq.at[mine, part],
                send_sem=send_in.at[4 + which],
                recv_sem=recv_q.at[plane],
                device_id=(there, frame),
                device_id_type=MESH,
            ).start()
            return carry

        lax.fori_loop(0, HEADS - 1, send, 0)

    copies = []

    def forward(which):
        buffer, part = window[which][1:]
        sides = ((0, HALO, HALO + ROWS, prv), (2, ROWS, 0, nxt))
        for side, (edge, start, landing, other) in enumerate(sides):
            arrived(buffer.at[pl.ds(start, HALO), part], recv_kv.at[which, edge])
            copy = pltpu.make_async_remote_copy(
                src_ref=buffer.at[pl.ds(start, HALO), part],
                dst_ref=buffer.at[pl.ds(landing, HALO), part],
                send_sem=send_halo.at[which, side],
                recv_sem=recv_halo.at[which, side],
                device_id=(beside, other),
                device_id_type=MESH,
            )
            copy.start()
            copies.append(copy)

    send_window(0)
    send_window(1)
    forward(0)
    send_window(2)
    forward(1)
    send_window(3)
    forward(2)
    send_queries(0)
    forward(3)
    send_queries(1)
    for which, (source, part) in enumerate(queries):
        pltpu.make_async_copy(source.at[:, column(me)], qq.at[mine, part], recv_q.at[plane]).start()
    for which, (source, buffer, part) in enumerate(window):
        arrived(buffer.at[pl.ds(HALO + 2 * PLANE, 4 * PLANE), part], recv_kv.at[which, 1])
    for copy in copies:
        copy.wait_recv()
    fetch.wait()

    scale = HD**-0.5
    nt = (((1,), (1,)), ((), ()))
    nn = (((1,), (0,)), ((), ()))

    def block_of(step):
        turn = step // 2
        half = (turn + 1) // 2
        shift = jnp.where(lax.rem(turn, 2) == 1, PLANES // 2 - half, PLANES // 2 + half)
        there = lax.rem(plane + shift, PLANES)
        x_lo = lax.rem(lax.rem(me, 4) // 2 + step + 1, 2)
        block = there * 2 + x_lo
        return there, block

    def send_back(step, block, which):
        result = (out, tan)[which]
        home = column(me)
        for flip in (1, 0):
            owner = block * 2 + lax.rem(me + flip, 2)
            piece = pl.ds(pl.multiple_of(owner * TOK, TOK), TOK)

            def remote(owner=owner, piece=piece):
                pltpu.make_async_remote_copy(
                    src_ref=oo.at[which, piece, :],
                    dst_ref=result.at[:, home],
                    send_sem=send_out.at[which],
                    recv_sem=recv_out.at[which],
                    device_id=(owner, frame),
                    device_id_type=MESH,
                ).start()

            def local(piece=piece):
                pltpu.make_async_copy(
                    oo.at[which, piece, :], result.at[:, home], recv_out.at[which]
                ).start()

            if flip:
                remote()
            else:
                pl.when(step < BLOCKS - 1)(remote)
                pl.when(step == BLOCKS - 1)(local)

    def block_step(step, carry):
        there, block = block_of(step)
        rows = pl.ds(pl.multiple_of(block * BQ, BQ), BQ)

        @pl.when(lax.rem(step, 2) == 0)
        def _():
            arrived(qq.at[pl.ds(pl.multiple_of(there * PLANE, PLANE), PLANE), :], recv_q.at[there])

        both = qq[rows, :]
        q = qq[rows, second]
        wins = []
        for slot in range(WK):
            local = jnp.clip(nbr[slot, block] - frame * BLOCKS + HB, 0, BLOCKS + 2 * HB - 1)
            wins.append(pl.ds(local * BQ, BQ))
        scores = [
            lax.dot_general(q, kk[win, first], nt, preferred_element_type=jnp.float32) for win in wins
        ]
        most = functools.reduce(jnp.maximum, [jnp.max(s, axis=1, keepdims=True) for s in scores])
        weights = [jnp.exp2((s - most) * (scale * LOG2E)) for s in scores]
        inv = 1.0 / functools.reduce(jnp.add, [jnp.sum(p, axis=1, keepdims=True) for p in weights])
        mean = jnp.zeros((BQ, 1), jnp.float32)
        acc = jnp.zeros((BQ, 2 * HD), jnp.float32)
        acc_w = jnp.zeros((BQ, HD), jnp.float32)
        for p, win in zip(weights, wins):
            p = p * inv
            st = lax.dot_general(both, kk[win, :], nt, preferred_element_type=jnp.float32)
            w = p * (st * scale)
            mean += jnp.sum(w, axis=1, keepdims=True)
            v = vv[win, :]
            acc += lax.dot_general(p.astype(jnp.bfloat16), v, nn, preferred_element_type=jnp.float32)
            acc_w += lax.dot_general(
                w.astype(jnp.bfloat16), v[:, :HD], nn, preferred_element_type=jnp.float32
            )
        o = acc[:, :HD]
        t = acc[:, HD:] + acc_w - mean * o
        oo[0, rows, :] = o.astype(jnp.bfloat16)
        oo[1, rows, :] = t.astype(jnp.bfloat16)
        send_back(step, block, 0)
        return carry

    def tan_step(step, carry):
        send_back(step, block_of(step)[1], 1)
        return carry

    lax.fori_loop(0, BLOCKS, block_step, 0)
    lax.fori_loop(0, BLOCKS, tan_step, 0)

    for copy in copies:
        copy.wait_send()
    rest = pl.ds(0, (HEADS - 1) * HD)
    for which in range(6):
        arrived(out.at[:, rest], send_in.at[which])
    for which, result in enumerate((out, tan)):
        arrived(result.at[:, rest], send_out.at[which])
        arrived(result, recv_out.at[which])


def hand_on(out, tan, out_copy, tan_copy, sems):
    copies = [
        pltpu.make_async_copy(out, out_copy, sems.at[0]),
        pltpu.make_async_copy(tan, tan_copy, sems.at[1]),
    ]
    for copy in copies:
        copy.start()
    for copy in copies:
        copy.wait()


def per_device(query, keys, values, query_tan, keys_tan, values_tan, neighbors):
    shape = jax.ShapeDtypeStruct((TOK, HEADS * HD), jnp.bfloat16)
    hbm = pl.BlockSpec(memory_space=pl.ANY)
    dma = pltpu.SemaphoreType.DMA
    results = pl.pallas_call(
        kernel,
        out_shape=(pltpu.VMEM((TOK, HEADS * HD), jnp.bfloat16),) * 2,
        in_specs=[hbm] * 7,
        out_specs=(hbm, hbm),
        scratch_shapes=[
            pltpu.SMEM((WK, BLOCKS), jnp.int32),
            pltpu.VMEM((ROWS + 2 * HALO, 2 * HD), jnp.bfloat16),
            pltpu.VMEM((ROWS + 2 * HALO, 2 * HD), jnp.bfloat16),
            pltpu.VMEM((ROWS, 2 * HD), jnp.bfloat16),
            pltpu.VMEM((2, ROWS, HD), jnp.bfloat16),
            pltpu.SemaphoreType.REGULAR,
            dma,
            dma((6,)),
            dma((4, 3)),
            dma((PLANES,)),
            dma((4, 2)),
            dma((4, 2)),
            dma((2,)),
            dma((2,)),
        ],
        compiler_params=pltpu.CompilerParams(
            collective_id=0, has_side_effects=True, vmem_limit_bytes=56 << 20
        ),
        cost_estimate=pl.CostEstimate(
            flops=7 * 10**9, bytes_accessed=20 << 20, transcendentals=5 * 10**6
        ),
        name="attend",
    )(neighbors.T, query, keys, values, query_tan, keys_tan, values_tan)
    results = [pltpu.with_memory_space_constraint(result, pltpu.VMEM) for result in results]
    return pl.pallas_call(
        hand_on,
        out_shape=(shape, shape),
        in_specs=[pl.BlockSpec(memory_space=pltpu.VMEM)] * 2,
        out_specs=(hbm, hbm),
        scratch_shapes=[dma((2,))],
        name="hand_on",
    )(*results)


def solution(mesh):
    tokens = P(("frames", "heads"), None)
    return jax.shard_map(
        per_device,
        mesh=mesh,
        in_specs=(tokens,) * 6 + (P("frames", None),),
        out_specs=(tokens, tokens),
        check_vma=False,
    )
```
